32 devices in a mesh: section: 4 (over y, x), seq: 8 (over z, core).
Axes of the slice: x: 2, y: 2, z: 4, core: 2. Of those that a mesh axis runs over, the one named last changes fastest.
Arguments:
- hidden: bfloat16 [4096, 4096], P('seq', 'section'), may hold values from -6 to 6
- norm_gain: bfloat16 [4096], P('section'), may hold values from 0.25 to 1.75
- query_weight: bfloat16 [4096, 512], P(None, 'section')
- key_weight: bfloat16 [4096, 128], P('section')
- value_weight: bfloat16 [4096, 128], P('section'), may hold values from -0.5 to 0.5
- output_weight: bfloat16 [512, 4096], P(None, 'section'), may hold values from -0.25 to 0.25
- block_reach: int32 [32], P('seq'), may hold values from 0 to 2
- header_ids: int32 [2], replicated, may hold values from 0 to 31, as said below
Outputs:
- attention_out: bfloat16 [4096, 4096], P('seq', 'section')
The draws below stay inside these ranges and needn't reach their ends.
Inputs may be any that keep to these rules, and one draw needn't show every extreme that they name: `header_ids`: the 2 indices are distinct block indices, and the last block, 31, is always one of them, at any position.
All inputs are finite; a program needn't handle non-finite values.
Results may differ from the reference program's by a relative error of at most 0.014.
Values may be sent and summed in bfloat16 or wider, within the bound.
A program may use at most 64 MiB of HBM per device.

```python
import math
import jax
import jax.numpy as jnp
from jax import lax

D = 4096
HEAD_DIM = 128
GROUP = 4
BLOCK = 128
REACH = 2
HEADER_BLOCKS = 2
BLOCKS_DEV = 4
ROWS = 512
NBLOCKS = 32
SEQ = 4096
N_SEQ = 8


def draw_query_weight(key, part):
    jitter = jax.random.normal(jax.random.fold_in(key, 12), (D, GROUP * HEAD_DIM), jnp.float32) * (1.0 / math.sqrt(D))
    return jitter.astype(jnp.bfloat16)


def draw_key_weight(key, part):
    jitter = jax.random.normal(jax.random.fold_in(key, 13), (D, HEAD_DIM), jnp.float32) * (2.0 / math.sqrt(D))
    return jitter.astype(jnp.bfloat16)


def draw_header_ids(key, part):
    others = jax.random.permutation(jax.random.fold_in(key, 17), NBLOCKS - 1)[:HEADER_BLOCKS - 1].astype(jnp.int32)
    chosen = jnp.concatenate([others, jnp.full((1,), NBLOCKS - 1, jnp.int32)])
    order = jax.random.permutation(jax.random.fold_in(key, 19), HEADER_BLOCKS).astype(jnp.int32)
    return jnp.take(chosen, order).astype(jnp.int32)


def set_ends(entries, key, low, high):
    longest = entries.shape.index(max(entries.shape))
    spots = []
    for shift in (0, 1):
        where = [jax.random.randint(jax.random.fold_in(key, axis), (), 0, length) for axis, length in enumerate(entries.shape)]
        where[longest] = (where[longest] + shift) % entries.shape[longest]
        spots.append(tuple(where))
    return entries.at[spots[0]].set(low).at[spots[1]].set(high)


def block_levels(rng, shape, cuts, low, high):
    gain = 1.0
    for axis_at, shards_of in cuts:
        steps = jax.random.uniform(jax.random.fold_in(jax.random.fold_in(rng, 6), axis_at), (shards_of,), jnp.float32, low / len(cuts), high / len(cuts))
        gain = gain * jnp.repeat(jnp.exp(steps), shape[axis_at] // shards_of).reshape((-1,) + (1,) * (len(shape) - 1 - axis_at))
    return gain


def centred(key, shape, spread, limit, cuts=(), held_as=jnp.bfloat16):
    values = spread * jax.random.normal(key, shape, jnp.float32)
    if cuts:
        values = values * block_levels(key, shape, cuts, -0.22, 0.18)
    return jnp.clip(values, -limit, limit).astype(held_as)


def setup_inputs(seed: int = 0) -> dict:
    key_list = jax.random.split(jax.random.key(seed), 9)
    return {
        "hidden": centred(key_list[0], (SEQ, D), 1.0, 6.0, ((0, 8), (1, 4))),
        "norm_gain": jnp.clip(1.0 + 0.15 * jax.random.normal(key_list[1], (D,), jnp.float32), 0.25, 1.75).astype(jnp.bfloat16),
        "query_weight": draw_query_weight(jax.random.fold_in(key_list[8], 71), 0),
        "key_weight": draw_key_weight(jax.random.fold_in(key_list[8], 71), 0),
        "value_weight": centred(key_list[4], (D, HEAD_DIM), (D // 32) ** -0.5, 0.5, ((0, 4),)),
        "output_weight": centred(key_list[5], (GROUP * HEAD_DIM, D), (GROUP * HEAD_DIM) ** -0.5, 0.25, ((1, 4),)),
        "block_reach": set_ends(jax.random.randint(key_list[6], (NBLOCKS,), 0, REACH + 1), jax.random.fold_in(key_list[6], 1), 0, REACH).astype(jnp.int32),
        "header_ids": draw_header_ids(jax.random.fold_in(key_list[8], 71), 0),
    }


EPSILON = 1e-05
THETA = 500000.0

def tables(positions, head_width):
    middle = head_width // 2
    frequency = jnp.exp(-(2.0 / head_width) * math.log(THETA) * jnp.arange(middle, dtype=jnp.float32))
    angles = positions.astype(jnp.float32)[:, None] * frequency[None, :]
    angles = jnp.concatenate([angles, angles], axis=1)
    return (jnp.cos(angles), jnp.sin(angles))

def rotate(values, cosine_table, sine_table):
    middle = values.shape[-1] // 2
    turned = jnp.concatenate([-values[..., middle:], values[..., :middle]], axis=-1)
    return values * cosine_table + turned * sine_table

def reference(hidden, norm_gain, query_weight, key_weight, value_weight, output_weight, block_reach, header_ids):
    floats = hidden.astype(jnp.float32)
    scaling = lax.rsqrt(lax.optimization_barrier(jnp.mean(floats * floats, axis=1, keepdims=True)) + EPSILON)
    normed = (floats * scaling * norm_gain.astype(jnp.float32)[None, :]).astype(jnp.bfloat16)
    positions = jnp.arange(SEQ, dtype=jnp.int32)
    cosine_table, sine_table = tables(positions, HEAD_DIM)
    queries = jnp.dot(normed, query_weight, preferred_element_type=jnp.float32).reshape(SEQ, GROUP, HEAD_DIM)
    queries = rotate(queries, cosine_table[:, None, :], sine_table[:, None, :]).astype(jnp.bfloat16)
    keys_all = rotate(jnp.dot(normed, key_weight, preferred_element_type=jnp.float32), cosine_table, sine_table).astype(jnp.bfloat16)
    values_all = jnp.dot(normed, value_weight, preferred_element_type=jnp.float32).astype(jnp.bfloat16)
    header_rows = (header_ids[:, None] * BLOCK + jnp.arange(BLOCK, dtype=jnp.int32)[None, :]).reshape(-1)
    head_queries = queries[header_rows].astype(jnp.float32)
    head_keys = keys_all[header_rows].astype(jnp.float32)
    head_values = values_all[header_rows].astype(jnp.float32)
    inverse_root = 1.0 / math.sqrt(HEAD_DIM)

    def shard_partial(shard_number):
        first_row = (shard_number * ROWS).astype(jnp.int32)
        shard_keys = lax.dynamic_slice_in_dim(keys_all, first_row, ROWS, 0).astype(jnp.float32)
        shard_values = lax.dynamic_slice_in_dim(values_all, first_row, ROWS, 0).astype(jnp.float32)
        scores = jnp.einsum('qgd,kd->gqk', head_queries, shard_keys) * inverse_root
        largest = lax.optimization_barrier(jnp.max(scores, axis=2))
        weights = jnp.exp(scores - largest[:, :, None])
        totals = lax.optimization_barrier(jnp.sum(weights, axis=2))
        rounded = lax.optimization_barrier(weights.astype(jnp.bfloat16)).astype(jnp.float32)
        partial_out = jnp.einsum('gqk,kd->gqd', rounded, shard_values)
        return (largest, totals, partial_out)
    largest, totals, partial_out = lax.map(shard_partial, jnp.arange(N_SEQ, dtype=jnp.int32))
    overall = lax.optimization_barrier(jnp.max(largest, axis=0))
    factors = jnp.exp(largest - overall[None])
    header_out = lax.optimization_barrier(jnp.sum(partial_out * factors[..., None], axis=0)) / lax.optimization_barrier(jnp.sum(totals * factors, axis=0))[..., None]
    margin_rows = REACH * BLOCK
    padded_keys = jnp.pad(keys_all, ((margin_rows, margin_rows), (0, 0)))
    padded_values = jnp.pad(values_all, ((margin_rows, margin_rows), (0, 0)))
    extent = ROWS + 2 * margin_rows

    def shard_window(shard_number):
        first_row = (shard_number * ROWS).astype(jnp.int32)
        near_keys = lax.dynamic_slice_in_dim(padded_keys, first_row, extent, 0).astype(jnp.float32)
        near_values = lax.dynamic_slice_in_dim(padded_values, first_row, extent, 0).astype(jnp.float32)
        key_blocks = shard_number * BLOCKS_DEV - REACH + jnp.arange(extent, dtype=jnp.int32) // BLOCK
        query_blocks = shard_number * BLOCKS_DEV + jnp.arange(ROWS, dtype=jnp.int32) // BLOCK
        limits = block_reach[query_blocks]
        key_header = jnp.any(header_ids[:, None] == key_blocks[None, :], axis=0)
        allowed = (key_blocks >= 0)[None, :] & (key_blocks < NBLOCKS)[None, :]
        allowed = allowed & (jnp.abs(key_blocks[None, :] - query_blocks[:, None]) <= limits[:, None])
        allowed = allowed & jnp.logical_not(key_header)[None, :]
        shard_queries = lax.dynamic_slice_in_dim(queries, first_row, ROWS, 0).astype(jnp.float32)
        near_scores = jnp.einsum('qgd,kd->gqk', shard_queries, near_keys) * inverse_root
        near_scores = jnp.where(allowed[None], near_scores, -jnp.inf)
        far_scores = jnp.einsum('qgd,kd->gqk', shard_queries, head_keys) * inverse_root
        scores = jnp.concatenate([near_scores, far_scores], axis=2)
        row_top = lax.optimization_barrier(jnp.max(scores, axis=2))
        weights = jnp.exp(scores - row_top[..., None])
        row_sums = lax.optimization_barrier(jnp.sum(weights, axis=2))
        rounded = lax.optimization_barrier(weights.astype(jnp.bfloat16)).astype(jnp.float32)
        joined = jnp.concatenate([near_values, head_values], axis=0)
        return jnp.einsum('gqk,kd->qgd', rounded, joined) / jnp.transpose(row_sums)[:, :, None]
    window = lax.map(shard_window, jnp.arange(N_SEQ, dtype=jnp.int32))
    window = window.reshape(NBLOCKS, BLOCK, GROUP, HEAD_DIM)
    header_blocks = jnp.transpose(header_out, (1, 0, 2)).reshape(HEADER_BLOCKS, BLOCK, GROUP, HEAD_DIM)
    window = window.at[header_ids].set(header_blocks)
    attended = window.reshape(SEQ, GROUP * HEAD_DIM).astype(jnp.bfloat16)
    return jnp.dot(attended, output_weight, preferred_element_type=jnp.float32).astype(jnp.bfloat16)
```

```python
import functools
import math

import jax
import jax.numpy as jnp
from jax import lax
from jax.experimental import pallas as pl
from jax.experimental.pallas import tpu as pltpu
from jax.sharding import PartitionSpec as P

BLOCK = 128
REACH = 2


EPSILON = 1e-05
THETA = 500000.0


def merged(value, axis, combine):
    everything = jax.tree.map(lambda part: lax.all_gather(part, axis), value)
    leading = jax.tree.map(lambda part: part[0], everything)

    def lap(k, so_far):
        return combine(so_far, jax.tree.map(lambda part: part[k], everything))

    return lax.fori_loop(1, lax.axis_size(axis), lap, leading)


def padded(cells, sides, width):
    for axis, dim in sides:
        count = lax.axis_size(axis)
        ends = count - 1
        head = lax.slice_in_dim(cells, 0, width, axis=dim)
        tail = lax.slice_in_dim(cells, cells.shape[dim] - width, cells.shape[dim], axis=dim)
        cells = jnp.concatenate(
            [
                lax.ppermute(tail, axis, [(i, (i + 1) % count) for i in range(ends)]),
                cells,
                lax.ppermute(head, axis, [((i + 1) % count, i) for i in range(ends)]),
            ],
            axis=dim,
        )
    return cells


def tables(positions, head_width):
    middle = head_width // 2
    frequency = jnp.exp(
        -(2.0 / head_width) * math.log(THETA) * jnp.arange(middle, dtype=jnp.float32)
    )
    angles = positions.astype(jnp.float32)[:, None] * frequency[None, :]
    angles = jnp.concatenate([angles, angles], axis=1)
    return (jnp.cos(angles), jnp.sin(angles))


def rotate(values, cosine_table, sine_table):
    middle = values.shape[-1] // 2
    turned = jnp.concatenate([-values[..., middle:], values[..., :middle]], axis=-1)
    return values * cosine_table + turned * sine_table


def combine_parts(earlier, later):
    first_max, first_total, first_out = earlier
    second_max, second_total, second_out = later
    overall = jnp.maximum(first_max, second_max)
    first_factor = jnp.exp(first_max - overall)
    second_factor = jnp.exp(second_max - overall)
    return (
        overall,
        first_total * first_factor + second_total * second_factor,
        first_out * first_factor[:, None] + second_out * second_factor[:, None],
    )


def on_device(
    hidden,
    norm_gain,
    query_weight,
    key_weight,
    value_weight,
    output_weight,
    block_reach,
    header_ids,
):
    row_count = hidden.shape[0]
    part_width = hidden.shape[1]
    head_width = key_weight.shape[1]
    local_blocks = row_count // BLOCK
    total_blocks = local_blocks * lax.axis_size("seq")
    seq_place = lax.axis_index("seq")
    floats = hidden.astype(jnp.float32)
    squares = lax.psum(jnp.sum(floats * floats, axis=1), "section")
    scaling = lax.rsqrt(squares / (part_width * lax.axis_size("section")) + EPSILON)
    normed_part = (floats * scaling[:, None] * norm_gain.astype(jnp.float32)[None, :]).astype(
        jnp.bfloat16
    )
    weight_rows = query_weight
    query_sum = jnp.dot(
        lax.all_gather(normed_part, "section", axis=1, tiled=True),
        weight_rows,
        preferred_element_type=jnp.float32,
    )
    key_sum, value_sum = lax.psum(
        (
            jnp.dot(normed_part, key_weight, preferred_element_type=jnp.float32),
            jnp.dot(normed_part, value_weight, preferred_element_type=jnp.float32),
        ),
        "section",
    )
    positions = seq_place * row_count + jnp.arange(row_count, dtype=jnp.int32)
    cosine_table, sine_table = tables(positions, head_width)
    queries = rotate(query_sum, cosine_table, sine_table).astype(jnp.bfloat16)
    keys_here = rotate(key_sum, cosine_table, sine_table).astype(jnp.bfloat16)
    values_here = value_sum.astype(jnp.bfloat16)
    packed = jnp.concatenate([queries, keys_here, values_here], axis=1)
    block_numbers = seq_place * local_blocks + jnp.arange(local_blocks, dtype=jnp.int32)
    select = header_ids[:, None] == block_numbers[None, :]
    shaped = packed.reshape(local_blocks, BLOCK, 3 * head_width)
    picked = jnp.einsum(
        "hb,bre->hre", select.astype(jnp.bfloat16), shaped, preferred_element_type=jnp.float32
    )
    header_pack = lax.psum(picked, "seq").astype(jnp.bfloat16).reshape(-1, 3 * head_width)
    head_queries = header_pack[:, :head_width]
    head_keys = header_pack[:, head_width : 2 * head_width]
    head_values = header_pack[:, 2 * head_width :]
    inverse_root = 1.0 / math.sqrt(head_width)
    far_scores = (
        jnp.einsum("qd,kd->qk", head_queries, keys_here, preferred_element_type=jnp.float32)
        * inverse_root
    )
    far_max = jnp.max(far_scores, axis=1)
    far_weights = jnp.exp(far_scores - far_max[:, None])
    far_total = jnp.sum(far_weights, axis=1)
    far_out = jnp.dot(
        far_weights.astype(jnp.bfloat16), values_here, preferred_element_type=jnp.float32
    )
    merged_max, merged_total, merged_out = merged(
        (far_max, far_total, far_out), "seq", combine_parts
    )
    header_result = merged_out / merged_total[:, None]
    margin_rows = REACH * BLOCK
    stacked = jnp.concatenate([keys_here, values_here], axis=1)
    extended = padded(stacked, (("seq", 0),), margin_rows)
    near_keys = extended[:, :head_width]
    near_values = extended[:, head_width:]
    extent = row_count + 2 * margin_rows
    key_blocks = seq_place * local_blocks - REACH + jnp.arange(extent, dtype=jnp.int32) // BLOCK
    query_blocks = seq_place * local_blocks + jnp.arange(row_count, dtype=jnp.int32) // BLOCK
    limits = jnp.repeat(block_reach, BLOCK)
    key_header = jnp.any(header_ids[:, None] == key_blocks[None, :], axis=0)
    allowed = (key_blocks >= 0)[None, :] & (key_blocks < total_blocks)[None, :]
    allowed = allowed & (jnp.abs(key_blocks[None, :] - query_blocks[:, None]) <= limits[:, None])
    allowed = allowed & jnp.logical_not(key_header)[None, :]
    near_scores = (
        jnp.einsum("qd,kd->qk", queries, near_keys, preferred_element_type=jnp.float32)
        * inverse_root
    )
    near_scores = jnp.where(allowed, near_scores, -jnp.inf)
    head_scores = (
        jnp.einsum("qd,kd->qk", queries, head_keys, preferred_element_type=jnp.float32)
        * inverse_root
    )
    scores = jnp.concatenate([near_scores, head_scores], axis=1)
    row_top = jnp.max(scores, axis=1)
    weights = jnp.exp(scores - row_top[:, None])
    row_sums = jnp.sum(weights, axis=1)
    joined = jnp.concatenate([near_values, head_values], axis=0)
    mixed_out = (
        jnp.dot(weights.astype(jnp.bfloat16), joined, preferred_element_type=jnp.float32)
        / row_sums[:, None]
    )
    header_local = jnp.einsum(
        "hb,hre->bre", select.astype(jnp.float32), header_result.reshape(-1, BLOCK, head_width)
    )
    is_local_header = jnp.any(select, axis=0)
    attended = jnp.where(
        is_local_header[:, None, None],
        header_local,
        mixed_out.reshape(local_blocks, BLOCK, head_width),
    )
    attended = attended.reshape(row_count, head_width).astype(jnp.bfloat16)
    weight_rows = output_weight
    result = jnp.dot(
        lax.all_gather(attended, "section", axis=1, tiled=True),
        weight_rows,
        preferred_element_type=jnp.float32,
    )
    return result.astype(jnp.bfloat16)


MESH = pl.DeviceIdType.MESH
LOW = -1e30
FUSED_BLOCKS = 64


def fused(
    n_section,
    n_line,
    hidden_ref,
    gain_ref,
    query_ref,
    key_ref,
    value_ref,
    cos_ref,
    sin_ref,
    reach_ref,
    ids_ref,
    out_ref,
    x,
    normed,
    wq,
    wkv,
    squares,
    kv_part,
    kv_got,
    q_part,
    q_got,
    blocks,
    queries,
    top,
    total,
    acc,
    local_sem,
    w_send,
    w_recv,
    wf_send,
    wf_recv,
    sq_send,
    sq_recv,
    kv_send,
    kv_recv,
    q_send,
    q_recv,
    line_send,
    plane_send,
    twin_send,
    block_recv,
    out_send,
    out_recv,
):
    width = x.shape[1]
    half = width // 2
    head = wq.shape[2]
    s = lax.axis_index("section")
    j = lax.axis_index("seq")
    z = j // 2
    c = j % 2
    twin = z * 2 + (1 - c)
    others = [(s + k) % n_section for k in range(1, n_section)]
    line = [((z + k) % n_line) * 2 + c for k in range(1, n_line)]

    def push(src, dst, send, recv, section, seq):
        copy = pltpu.make_async_remote_copy(
            src_ref=src,
            dst_ref=dst,
            send_sem=send,
            recv_sem=recv,
            device_id=(section, seq),
            device_id_type=MESH,
        )
        copy.start()
        pending.append(copy)

    def arrived(dst, recv):
        pltpu.make_async_remote_copy(
            src_ref=dst,
            dst_ref=dst,
            send_sem=local_sem.at[4],
            recv_sem=recv,
            device_id=(s, twin),
            device_id_type=MESH,
        ).wait_recv()

    pending = []
    get_x = pltpu.make_async_copy(hidden_ref, x, local_sem.at[0])
    get_k = pltpu.make_async_copy(key_ref, wkv.at[:, 0:head], local_sem.at[1])
    get_v = pltpu.make_async_copy(value_ref, wkv.at[:, head : 2 * head], local_sem.at[2])
    get_q = pltpu.make_async_copy(
        query_ref.at[pl.ds(pl.multiple_of(s * width, width), width), :], wq.at[s], local_sem.at[3]
    )
    get_x.start()
    get_k.start()
    get_v.start()
    get_q.start()

    barrier = pltpu.get_barrier_semaphore()
    friends = [(t, j) for t in others] + [(s, i) for i in line] + [(s, twin)]
    for friend in friends:
        pl.semaphore_signal(barrier, inc=1, device_id=friend, device_id_type=MESH)
    pl.semaphore_wait(barrier, len(friends))

    mine = pl.ds(pl.multiple_of(c * half, half), half)
    for k, t in enumerate(others):
        push(
            query_ref.at[pl.ds(pl.multiple_of(t * width + c * half, half), half), :],
            wq.at[s, mine, :],
            w_send.at[k],
            w_recv.at[s],
            t,
            j,
        )

    get_x.wait()
    for r in range(n_section):
        part = x[r * BLOCK : (r + 1) * BLOCK, :].astype(jnp.float32)
        column = jnp.sum(part * part, axis=1, keepdims=True)
        squares[s, r] = jnp.transpose(jnp.broadcast_to(column, (BLOCK, BLOCK)))[:8, :]
    for k, t in enumerate(others):
        push(squares.at[s], squares.at[s], sq_send.at[k], sq_recv.at[s], t, j)
    for t in others:
        arrived(squares.at[t], sq_recv.at[t])
    sums = squares[0]
    for t in range(1, n_section):
        sums = sums + squares[t]
    scaling = lax.rsqrt(sums / (width * n_section) + EPSILON)
    gain = gain_ref[...].astype(jnp.float32)
    for r in range(n_section):
        column = jnp.transpose(jnp.broadcast_to(scaling[r, 0:1, :], (BLOCK, BLOCK)))[:, 0:1]
        part = x[r * BLOCK : (r + 1) * BLOCK, :].astype(jnp.float32)
        normed[r * BLOCK : (r + 1) * BLOCK, :] = (part * column * gain).astype(jnp.bfloat16)

    get_k.wait()
    get_v.wait()
    kv_part[...] = (
        jnp.dot(normed[...], wkv[...], preferred_element_type=jnp.float32)
        .astype(jnp.bfloat16)
        .reshape(kv_part.shape)
    )
    for k, t in enumerate(others):
        push(kv_part.at[t], kv_got.at[s], kv_send.at[k], kv_recv.at[s], t, j)

    def project(k):
        owner = (s + k) % n_section
        q_part[k] = (
            jnp.dot(normed[...], wq[owner], preferred_element_type=jnp.float32)
            .astype(jnp.bfloat16)
            .reshape(q_part.shape[1:])
        )
        for i, t in enumerate(others):
            push(q_part.at[k, t], q_got.at[s, owner], q_send.at[k, i], q_recv.at[s, owner], t, j)

    get_q.wait()
    project(0)

    cosine = cos_ref[...]
    sine = sin_ref[...]

    def turned(values):
        return values * cosine + pltpu.roll(values, head // 2, axis=1) * sine

    b = j * n_section + s
    for t in others:
        arrived(kv_got.at[t], kv_recv.at[t])
    kv = kv_part[s].astype(jnp.float32)
    for t in others:
        kv = kv + kv_got[t].astype(jnp.float32)
    blocks[b, :, 0:head] = turned(kv[:, :head]).astype(jnp.bfloat16)
    blocks[b, :, head : 2 * head] = kv[:, head:].astype(jnp.bfloat16)

    def spread(number, slot):
        for k, t in enumerate(others):
            push(
                blocks.at[number],
                blocks.at[number],
                plane_send.at[slot, k],
                block_recv.at[number],
                t,
                j,
            )
        push(
            blocks.at[number], blocks.at[number], twin_send.at[slot, 0], block_recv.at[number], s, twin
        )

    for k, i in enumerate(line):
        push(blocks.at[b], blocks.at[b], line_send.at[k], block_recv.at[b], s, i)
    spread(b, 0)

    for k, t in enumerate(others):
        arrived(wq.at[t, mine, :], w_recv.at[t])
        push(wq.at[t, mine, :], wq.at[t, mine, :], wf_send.at[k], wf_recv.at[t], s, twin)
    theirs = pl.ds(pl.multiple_of((1 - c) * half, half), half)
    for k, t in enumerate(others):
        arrived(wq.at[t, theirs, :], wf_recv.at[t])
        project(k + 1)

    for k, i in enumerate(line):
        number = i * n_section + s
        arrived(blocks.at[number], block_recv.at[number])
        spread(number, k + 1)

    for t in others:
        for h in range(n_section):
            arrived(q_got.at[t, h], q_recv.at[t, h])
    for h in range(n_section):
        place = (h + n_section - s) % n_section
        value = q_part[place, s].astype(jnp.float32)
        for t in others:
            value = value + q_got[t, h].astype(jnp.float32)
        queries[h] = turned(value).astype(jnp.bfloat16)

    first = ids_ref[0]
    second = ids_ref[1]
    own_header = jnp.logical_or(first == b, second == b)
    limit = jnp.where(own_header, n_section * n_line * 2, reach_ref[s])
    group = n_section * BLOCK
    factor = 1.4426950408889634 / math.sqrt(head)
    top[...] = jnp.full(top.shape, LOW, jnp.float32)
    total[...] = jnp.zeros(total.shape, jnp.float32)
    acc[...] = jnp.zeros(acc.shape, jnp.float32)

    def attend(seq):
        start = seq * n_section
        numbers = start + lax.broadcasted_iota(jnp.int32, (1, group), 1) // BLOCK
        valid = (numbers == first) | (numbers == second) | (jnp.abs(numbers - b) <= limit)
        bias = jnp.where(valid, 0.0, LOW)
        keys = blocks[pl.ds(start, n_section), :, 0:head].reshape(group, head)
        values = blocks[pl.ds(start, n_section), :, head : 2 * head].reshape(group, head)
        for h in range(n_section):
            scores = lax.dot_general(
                queries[h], keys, (((1,), (1,)), ((), ())), preferred_element_type=jnp.float32
            )
            scores = scores * factor + bias
            before = top[h]
            after = jnp.maximum(before, jnp.max(scores, axis=1, keepdims=True))
            fade = jnp.exp2(before - after)
            weights = jnp.exp2(scores - after[:, 0:1])
            top[h] = after
            total[h] = total[h] * fade + jnp.sum(weights, axis=1, keepdims=True)
            acc[h] = acc[h] * fade + jnp.dot(
                weights.astype(jnp.bfloat16), values, preferred_element_type=jnp.float32
            )

    for i in range(n_line):
        seq = ((z + i) % n_line) * 2 + c
        for k, t in enumerate(others):
            number = seq * n_section + t
            arrived(blocks.at[number], block_recv.at[number])
            push(
                blocks.at[number],
                blocks.at[number],
                twin_send.at[i, k + 1],
                block_recv.at[number],
                s,
                twin,
            )
        attend(seq)
    for i in range(n_line):
        seq = ((z + i) % n_line) * 2 + (1 - c)
        for t in range(n_section):
            arrived(blocks.at[seq * n_section + t], block_recv.at[seq * n_section + t])
        attend(seq)

    for h in range(n_section):
        out_ref[s, :, h * head : (h + 1) * head] = (acc[h] / total[h]).astype(jnp.bfloat16)
    for k, t in enumerate(others):
        push(out_ref.at[s], out_ref.at[s], out_send.at[k], out_recv.at[s], t, j)
    for t in others:
        arrived(out_ref.at[t], out_recv.at[t])
    for copy in pending:
        copy.wait_send()


def on_device_fused(
    n_section,
    n_seq,
    hidden,
    norm_gain,
    query_weight,
    key_weight,
    value_weight,
    output_weight,
    block_reach,
    header_ids,
):
    rows, width = hidden.shape
    head = key_weight.shape[1]
    n_line = n_seq // 2
    n_blocks = n_section * n_seq
    first = lax.axis_index("seq") * rows + lax.axis_index("section") * BLOCK
    cosine, sine = tables(first + jnp.arange(BLOCK, dtype=jnp.int32), head)
    sine = jnp.concatenate([-sine[:, : head // 2], sine[:, head // 2 :]], axis=1)
    vmem = pl.BlockSpec(memory_space=pltpu.VMEM)
    smem = pl.BlockSpec(memory_space=pltpu.SMEM)
    anywhere = pl.BlockSpec(memory_space=pl.ANY)
    dma = pltpu.SemaphoreType.DMA
    bf16 = jnp.bfloat16
    f32 = jnp.float32
    attended = pl.pallas_call(
        functools.partial(fused, n_section, n_line),
        out_shape=jax.ShapeDtypeStruct((n_section, BLOCK, n_section * head), bf16),
        in_specs=[anywhere, vmem, anywhere, anywhere, anywhere, vmem, vmem, smem, smem],
        out_specs=vmem,
        scratch_shapes=[
            pltpu.VMEM((rows, width), bf16),
            pltpu.VMEM((rows, width), bf16),
            pltpu.VMEM((n_section, width, head), bf16),
            pltpu.VMEM((width, 2 * head), bf16),
            pltpu.VMEM((n_section, n_section, 8, BLOCK), f32),
            pltpu.VMEM((n_section, BLOCK, 2 * head), bf16),
            pltpu.VMEM((n_section, BLOCK, 2 * head), bf16),
            pltpu.VMEM((n_section, n_section, BLOCK, head), bf16),
            pltpu.VMEM((n_section, n_section, BLOCK, head), bf16),
            pltpu.VMEM((n_blocks, BLOCK, 2 * head), bf16),
            pltpu.VMEM((n_section, BLOCK, head), bf16),
            pltpu.VMEM((n_section, BLOCK, head), f32),
            pltpu.VMEM((n_section, BLOCK, head), f32),
            pltpu.VMEM((n_section, BLOCK, head), f32),
            dma((5,)),
            dma((n_section - 1,)),
            dma((n_section,)),
            dma((n_section - 1,)),
            dma((n_section,)),
            dma((n_section - 1,)),
            dma((n_section,)),
            dma((n_section - 1,)),
            dma((n_section,)),
            dma((n_section, n_section - 1)),
            dma((n_section, n_section)),
            dma((n_line - 1,)),
            dma((n_line, n_section - 1)),
            dma((n_line, n_section)),
            dma((n_blocks,)),
            dma((n_section - 1,)),
            dma((n_section,)),
        ],
        compiler_params=pltpu.CompilerParams(
            collective_id=0, has_side_effects=True, vmem_limit_bytes=40 * 1024 * 1024
        ),
    )(
        hidden,
        norm_gain.reshape(1, width),
        query_weight,
        key_weight,
        value_weight,
        cosine,
        sine,
        block_reach,
        header_ids,
    )
    return jnp.dot(
        attended.reshape(rows, n_section * head), output_weight, preferred_element_type=f32
    ).astype(bf16)


def solution(mesh):
    n_section, n_seq = mesh.shape["section"], mesh.shape["seq"]
    if n_section * n_seq <= FUSED_BLOCKS:
        program = functools.partial(on_device_fused, n_section, n_seq)
    else:
        program = on_device
    return jax.shard_map(
        program,
        mesh=mesh,
        in_specs=(
            P("seq", "section"),
            P("section"),
            P(None, "section"),
            P("section", None),
            P("section", None),
            P(None, "section"),
            P("seq"),
            P(),
        ),
        out_specs=P("seq", "section"),
        check_vma=False,
    )
```

```python
import functools
import math

import jax
import jax.numpy as jnp
from jax import lax
from jax.experimental import pallas as pl
from jax.experimental.pallas import tpu as pltpu
from jax.sharding import PartitionSpec as P

BLOCK = 128
REACH = 2


EPSILON = 1e-05
THETA = 500000.0


def merged(value, axis, combine):
    everything = jax.tree.map(lambda part: lax.all_gather(part, axis), value)
    leading = jax.tree.map(lambda part: part[0], everything)

    def lap(k, so_far):
        return combine(so_far, jax.tree.map(lambda part: part[k], everything))

    return lax.fori_loop(1, lax.axis_size(axis), lap, leading)


def padded(cells, sides, width):
    for axis, dim in sides:
        count = lax.axis_size(axis)
        ends = count - 1
        head = lax.slice_in_dim(cells, 0, width, axis=dim)
        tail = lax.slice_in_dim(cells, cells.shape[dim] - width, cells.shape[dim], axis=dim)
        cells = jnp.concatenate(
            [
                lax.ppermute(tail, axis, [(i, (i + 1) % count) for i in range(ends)]),
                cells,
                lax.ppermute(head, axis, [((i + 1) % count, i) for i in range(ends)]),
            ],
            axis=dim,
        )
    return cells


def tables(positions, head_width):
    middle = head_width // 2
    frequency = jnp.exp(
        -(2.0 / head_width) * math.log(THETA) * jnp.arange(middle, dtype=jnp.float32)
    )
    angles = positions.astype(jnp.float32)[:, None] * frequency[None, :]
    angles = jnp.concatenate([angles, angles], axis=1)
    return (jnp.cos(angles), jnp.sin(angles))


def rotate(values, cosine_table, sine_table):
    middle = values.shape[-1] // 2
    turned = jnp.concatenate([-values[..., middle:], values[..., :middle]], axis=-1)
    return values * cosine_table + turned * sine_table


def combine_parts(earlier, later):
    first_max, first_total, first_out = earlier
    second_max, second_total, second_out = later
    overall = jnp.maximum(first_max, second_max)
    first_factor = jnp.exp(first_max - overall)
    second_factor = jnp.exp(second_max - overall)
    return (
        overall,
        first_total * first_factor + second_total * second_factor,
        first_out * first_factor[:, None] + second_out * second_factor[:, None],
    )


def on_device(
    hidden,
    norm_gain,
    query_weight,
    key_weight,
    value_weight,
    output_weight,
    block_reach,
    header_ids,
):
    row_count = hidden.shape[0]
    part_width = hidden.shape[1]
    head_width = key_weight.shape[1]
    local_blocks = row_count // BLOCK
    total_blocks = local_blocks * lax.axis_size("seq")
    seq_place = lax.axis_index("seq")
    floats = hidden.astype(jnp.float32)
    squares = lax.psum(jnp.sum(floats * floats, axis=1), "section")
    scaling = lax.rsqrt(squares / (part_width * lax.axis_size("section")) + EPSILON)
    normed_part = (floats * scaling[:, None] * norm_gain.astype(jnp.float32)[None, :]).astype(
        jnp.bfloat16
    )
    weight_rows = query_weight
    query_sum = jnp.dot(
        lax.all_gather(normed_part, "section", axis=1, tiled=True),
        weight_rows,
        preferred_element_type=jnp.float32,
    )
    key_sum, value_sum = lax.psum(
        (
            jnp.dot(normed_part, key_weight, preferred_element_type=jnp.float32),
            jnp.dot(normed_part, value_weight, preferred_element_type=jnp.float32),
        ),
        "section",
    )
    positions = seq_place * row_count + jnp.arange(row_count, dtype=jnp.int32)
    cosine_table, sine_table = tables(positions, head_width)
    queries = rotate(query_sum, cosine_table, sine_table).astype(jnp.bfloat16)
    keys_here = rotate(key_sum, cosine_table, sine_table).astype(jnp.bfloat16)
    values_here = value_sum.astype(jnp.bfloat16)
    packed = jnp.concatenate([queries, keys_here, values_here], axis=1)
    block_numbers = seq_place * local_blocks + jnp.arange(local_blocks, dtype=jnp.int32)
    select = header_ids[:, None] == block_numbers[None, :]
    shaped = packed.reshape(local_blocks, BLOCK, 3 * head_width)
    picked = jnp.einsum(
        "hb,bre->hre", select.astype(jnp.bfloat16), shaped, preferred_element_type=jnp.float32
    )
    header_pack = lax.psum(picked, "seq").astype(jnp.bfloat16).reshape(-1, 3 * head_width)
    head_queries = header_pack[:, :head_width]
    head_keys = header_pack[:, head_width : 2 * head_width]
    head_values = header_pack[:, 2 * head_width :]
    inverse_root = 1.0 / math.sqrt(head_width)
    far_scores = (
        jnp.einsum("qd,kd->qk", head_queries, keys_here, preferred_element_type=jnp.float32)
        * inverse_root
    )
    far_max = jnp.max(far_scores, axis=1)
    far_weights = jnp.exp(far_scores - far_max[:, None])
    far_total = jnp.sum(far_weights, axis=1)
    far_out = jnp.dot(
        far_weights.astype(jnp.bfloat16), values_here, preferred_element_type=jnp.float32
    )
    merged_max, merged_total, merged_out = merged(
        (far_max, far_total, far_out), "seq", combine_parts
    )
    header_result = merged_out / merged_total[:, None]
    margin_rows = REACH * BLOCK
    stacked = jnp.concatenate([keys_here, values_here], axis=1)
    extended = padded(stacked, (("seq", 0),), margin_rows)
    near_keys = extended[:, :head_width]
    near_values = extended[:, head_width:]
    extent = row_count + 2 * margin_rows
    key_blocks = seq_place * local_blocks - REACH + jnp.arange(extent, dtype=jnp.int32) // BLOCK
    query_blocks = seq_place * local_blocks + jnp.arange(row_count, dtype=jnp.int32) // BLOCK
    limits = jnp.repeat(block_reach, BLOCK)
    key_header = jnp.any(header_ids[:, None] == key_blocks[None, :], axis=0)
    allowed = (key_blocks >= 0)[None, :] & (key_blocks < total_blocks)[None, :]
    allowed = allowed & (jnp.abs(key_blocks[None, :] - query_blocks[:, None]) <= limits[:, None])
    allowed = allowed & jnp.logical_not(key_header)[None, :]
    near_scores = (
        jnp.einsum("qd,kd->qk", queries, near_keys, preferred_element_type=jnp.float32)
        * inverse_root
    )
    near_scores = jnp.where(allowed, near_scores, -jnp.inf)
    head_scores = (
        jnp.einsum("qd,kd->qk", queries, head_keys, preferred_element_type=jnp.float32)
        * inverse_root
    )
    scores = jnp.concatenate([near_scores, head_scores], axis=1)
    row_top = jnp.max(scores, axis=1)
    weights = jnp.exp(scores - row_top[:, None])
    row_sums = jnp.sum(weights, axis=1)
    joined = jnp.concatenate([near_values, head_values], axis=0)
    mixed_out = (
        jnp.dot(weights.astype(jnp.bfloat16), joined, preferred_element_type=jnp.float32)
        / row_sums[:, None]
    )
    header_local = jnp.einsum(
        "hb,hre->bre", select.astype(jnp.float32), header_result.reshape(-1, BLOCK, head_width)
    )
    is_local_header = jnp.any(select, axis=0)
    attended = jnp.where(
        is_local_header[:, None, None],
        header_local,
        mixed_out.reshape(local_blocks, BLOCK, head_width),
    )
    attended = attended.reshape(row_count, head_width).astype(jnp.bfloat16)
    weight_rows = output_weight
    result = jnp.dot(
        lax.all_gather(attended, "section", axis=1, tiled=True),
        weight_rows,
        preferred_element_type=jnp.float32,
    )
    return result.astype(jnp.bfloat16)


MESH = pl.DeviceIdType.MESH
LOW = -1e30
FUSED_BLOCKS = 64


def fused(
    n_section,
    n_line,
    hidden_ref,
    gain_ref,
    query_ref,
    key_ref,
    value_ref,
    reach_ref,
    ids_ref,
    out_ref,
    x,
    normed,
    wq,
    wkv,
    squares,
    kv_part,
    kv_got,
    q_part,
    q_got,
    blocks,
    queries,
    top,
    total,
    acc,
    local_sem,
    x_sem,
    w_send,
    w_recv,
    wf_send,
    wf_recv,
    sq_send,
    sq_recv,
    kv_send,
    kv_recv,
    q_send,
    q_recv,
    line_send,
    plane_send,
    twin_send,
    block_recv,
    out_send,
    out_recv,
):
    width = x.shape[1]
    half = width // 2
    head = wq.shape[2]
    s = lax.axis_index("section")
    j = lax.axis_index("seq")
    z = j // 2
    c = j % 2
    twin = z * 2 + (1 - c)
    others = [(s + k) % n_section for k in range(1, n_section)]
    line = [((z + k) % n_line) * 2 + c for k in range(1, n_line)]

    def push(src, dst, send, recv, section, seq):
        copy = pltpu.make_async_remote_copy(
            src_ref=src,
            dst_ref=dst,
            send_sem=send,
            recv_sem=recv,
            device_id=(section, seq),
            device_id_type=MESH,
        )
        copy.start()
        pending.append(copy)

    def arrived(dst, recv):
        pltpu.make_async_remote_copy(
            src_ref=dst,
            dst_ref=dst,
            send_sem=local_sem.at[4],
            recv_sem=recv,
            device_id=(s, twin),
            device_id_type=MESH,
        ).wait_recv()

    pending = []
    get_x = []
    for r in range(n_section):
        rows = pl.ds(r * BLOCK, BLOCK)
        get_x.append(pltpu.make_async_copy(hidden_ref.at[rows, :], x.at[rows, :], x_sem.at[r]))
        get_x[r].start()
    get_k = pltpu.make_async_copy(key_ref, wkv.at[:, 0:head], local_sem.at[1])
    get_v = pltpu.make_async_copy(value_ref, wkv.at[:, head : 2 * head], local_sem.at[2])
    get_q = pltpu.make_async_copy(
        query_ref.at[pl.ds(pl.multiple_of(s * width, width), width), :], wq.at[s], local_sem.at[3]
    )
    get_k.start()
    get_v.start()
    get_q.start()

    barrier = pltpu.get_barrier_semaphore()
    friends = [(t, j) for t in others] + [(s, i) for i in line] + [(s, twin)]
    for friend in friends:
        pl.semaphore_signal(barrier, inc=1, device_id=friend, device_id_type=MESH)
    pl.semaphore_wait(barrier, len(friends))

    mine = pl.ds(pl.multiple_of(c * half, half), half)
    for k, t in enumerate(others):
        push(
            query_ref.at[pl.ds(pl.multiple_of(t * width + c * half, half), half), :],
            wq.at[s, mine, :],
            w_send.at[k],
            w_recv.at[s],
            t,
            j,
        )

    b = j * n_section + s
    lanes = lax.broadcasted_iota(jnp.int32, (BLOCK, head), 1)
    positions = b * BLOCK + lax.broadcasted_iota(jnp.int32, (BLOCK, head), 0)
    spots = lax.rem(lanes, head // 2).astype(jnp.float32)
    angles = positions.astype(jnp.float32) * jnp.exp(-(2.0 / head) * math.log(THETA) * spots)
    cosine = jnp.cos(angles)
    sine = jnp.where(lanes < head // 2, -1.0, 1.0) * jnp.sin(angles)

    for r in range(n_section):
        get_x[r].wait()
        part = x[r * BLOCK : (r + 1) * BLOCK, :].astype(jnp.float32)
        column = jnp.sum(part * part, axis=1, keepdims=True)
        squares[s, r] = jnp.transpose(jnp.broadcast_to(column, (BLOCK, BLOCK)))[:8, :]
    for k, t in enumerate(others):
        push(squares.at[s], squares.at[s], sq_send.at[k], sq_recv.at[s], t, j)
    for t in others:
        arrived(squares.at[t], sq_recv.at[t])
    sums = squares[0]
    for t in range(1, n_section):
        sums = sums + squares[t]
    scaling = lax.rsqrt(sums / (width * n_section) + EPSILON)
    gain = gain_ref[...].astype(jnp.float32).reshape(1, width)
    for r in range(n_section):
        column = jnp.transpose(jnp.broadcast_to(scaling[r, 0:1, :], (BLOCK, BLOCK)))[:, 0:1]
        part = x[r * BLOCK : (r + 1) * BLOCK, :].astype(jnp.float32)
        normed[r * BLOCK : (r + 1) * BLOCK, :] = (part * column * gain).astype(jnp.bfloat16)

    get_k.wait()
    get_v.wait()
    kv_part[...] = (
        jnp.dot(normed[...], wkv[...], preferred_element_type=jnp.float32)
        .astype(jnp.bfloat16)
        .reshape(kv_part.shape)
    )
    for k, t in enumerate(others):
        push(kv_part.at[t], kv_got.at[s], kv_send.at[k], kv_recv.at[s], t, j)

    def project(k):
        owner = (s + k) % n_section
        q_part[k] = (
            jnp.dot(normed[...], wq[owner], preferred_element_type=jnp.float32)
            .astype(jnp.bfloat16)
            .reshape(q_part.shape[1:])
        )
        for i, t in enumerate(others):
            push(q_part.at[k, t], q_got.at[s, owner], q_send.at[k, i], q_recv.at[s, owner], t, j)

    get_q.wait()
    project(0)
    for k, t in enumerate(others):
        arrived(wq.at[t, mine, :], w_recv.at[t])
        push(wq.at[t, mine, :], wq.at[t, mine, :], wf_send.at[k], wf_recv.at[t], s, twin)

    def turned(values):
        return values * cosine + pltpu.roll(values, head // 2, axis=1) * sine

    for t in others:
        arrived(kv_got.at[t], kv_recv.at[t])
    kv = kv_part[s].astype(jnp.float32)
    for t in others:
        kv = kv + kv_got[t].astype(jnp.float32)
    blocks[b, :, 0:head] = turned(kv[:, :head]).astype(jnp.bfloat16)
    blocks[b, :, head : 2 * head] = kv[:, head:].astype(jnp.bfloat16)

    across = s + 1 - 2 * (s % 2)
    along = (s + 2) % n_section
    corner = (across + 2) % n_section
    relayed = jnp.where(c == 0, across, along)
    direct = jnp.where(c == 0, along, across)

    def hand(number, send, section, seq):
        push(blocks.at[number], blocks.at[number], send, block_recv.at[number], section, seq)

    def spread(number, slot):
        hand(number, plane_send.at[slot, 0], relayed, j)
        hand(number, plane_send.at[slot, 1], direct, j)
        hand(number, twin_send.at[slot, 0], s, twin)

    for k, i in enumerate(line):
        push(blocks.at[b], blocks.at[b], line_send.at[k], block_recv.at[b], s, i)
    spread(b, 0)

    theirs = pl.ds(pl.multiple_of((1 - c) * half, half), half)
    for k, t in enumerate(others):
        arrived(wq.at[t, theirs, :], wf_recv.at[t])
        project(k + 1)

    for k, i in enumerate(line):
        number = i * n_section + s
        arrived(blocks.at[number], block_recv.at[number])
        spread(number, k + 1)
    for i, seq in enumerate([j] + line):
        number = seq * n_section + relayed
        arrived(blocks.at[number], block_recv.at[number])
        hand(number, plane_send.at[i, 2], direct, j)
        hand(number, twin_send.at[i, 1], s, twin)

    for t in others:
        for h in range(n_section):
            arrived(q_got.at[t, h], q_recv.at[t, h])
    for h in range(n_section):
        place = (h + n_section - s) % n_section
        value = q_part[place, s].astype(jnp.float32)
        for t in others:
            value = value + q_got[t, h].astype(jnp.float32)
        queries[h] = turned(value).astype(jnp.bfloat16)

    first = ids_ref[0]
    second = ids_ref[1]
    own_header = jnp.logical_or(first == b, second == b)
    limit = jnp.where(own_header, n_section * n_line * 2, reach_ref[s])
    group = n_section * BLOCK
    factor = 1.4426950408889634 / math.sqrt(head)
    top[...] = jnp.full(top.shape, LOW, jnp.float32)
    total[...] = jnp.zeros(total.shape, jnp.float32)
    acc[...] = jnp.zeros(acc.shape, jnp.float32)

    def attend(seq):
        start = seq * n_section
        numbers = start + lax.broadcasted_iota(jnp.int32, (1, group), 1) // BLOCK
        valid = (numbers == first) | (numbers == second) | (jnp.abs(numbers - b) <= limit)
        bias = jnp.where(valid, 0.0, LOW)
        keys = blocks[pl.ds(start, n_section), :, 0:head].reshape(group, head)
        values = blocks[pl.ds(start, n_section), :, head : 2 * head].reshape(group, head)
        for h in range(n_section):
            scores = lax.dot_general(
                queries[h], keys, (((1,), (1,)), ((), ())), preferred_element_type=jnp.float32
            )
            scores = scores * factor + bias
            before = top[h]
            after = jnp.maximum(before, jnp.max(scores, axis=1, keepdims=True))
            fade = jnp.exp2(before - after)
            weights = jnp.exp2(scores - after[:, 0:1])
            top[h] = after
            total[h] = total[h] * fade + jnp.sum(weights, axis=1, keepdims=True)
            acc[h] = acc[h] * fade + jnp.dot(
                weights.astype(jnp.bfloat16), values, preferred_element_type=jnp.float32
            )

    def attend_twin(i):
        seq = ((z + i) % n_line) * 2 + (1 - c)
        for t in range(n_section):
            arrived(blocks.at[seq * n_section + t], block_recv.at[seq * n_section + t])
        attend(seq)

    for i in range(n_line):
        seq = ((z + i) % n_line) * 2 + c
        for k, t in enumerate([direct, corner]):
            number = seq * n_section + t
            arrived(blocks.at[number], block_recv.at[number])
            hand(number, twin_send.at[i, k + 2], s, twin)
        attend(seq)
        if i > 0:
            attend_twin(i - 1)
    attend_twin(n_line - 1)

    for h in range(n_section):
        columns = pl.ds(h * head, head)
        out_ref[s, :, columns] = (acc[h] / total[h]).astype(jnp.bfloat16)
        piece = out_ref.at[s, :, columns]
        for k, t in enumerate(others):
            push(piece, piece, out_send.at[h, k], out_recv.at[s, h], t, j)
    for t in others:
        for h in range(n_section):
            arrived(out_ref.at[t, :, pl.ds(h * head, head)], out_recv.at[t, h])
    for copy in pending:
        copy.wait_send()


def on_device_fused(
    n_section,
    n_seq,
    hidden,
    norm_gain,
    query_weight,
    key_weight,
    value_weight,
    output_weight,
    block_reach,
    header_ids,
):
    rows, width = hidden.shape
    head = key_weight.shape[1]
    n_line = n_seq // 2
    n_blocks = n_section * n_seq
    vmem = pl.BlockSpec(memory_space=pltpu.VMEM)
    smem = pl.BlockSpec(memory_space=pltpu.SMEM)
    anywhere = pl.BlockSpec(memory_space=pltpu.HBM)
    dma = pltpu.SemaphoreType.DMA
    bf16 = jnp.bfloat16
    f32 = jnp.float32
    attended = pl.pallas_call(
        functools.partial(fused, n_section, n_line),
        out_shape=jax.ShapeDtypeStruct((n_section, BLOCK, n_section * head), bf16),
        in_specs=[anywhere, vmem, anywhere, anywhere, anywhere, smem, smem],
        out_specs=vmem,
        scratch_shapes=[
            pltpu.VMEM((rows, width), bf16),
            pltpu.VMEM((rows, width), bf16),
            pltpu.VMEM((n_section, width, head), bf16),
            pltpu.VMEM((width, 2 * head), bf16),
            pltpu.VMEM((n_section, n_section, 8, BLOCK), f32),
            pltpu.VMEM((n_section, BLOCK, 2 * head), bf16),
            pltpu.VMEM((n_section, BLOCK, 2 * head), bf16),
            pltpu.VMEM((n_section, n_section, BLOCK, head), bf16),
            pltpu.VMEM((n_section, n_section, BLOCK, head), bf16),
            pltpu.VMEM((n_blocks, BLOCK, 2 * head), bf16),
            pltpu.VMEM((n_section, BLOCK, head), bf16),
            pltpu.VMEM((n_section, BLOCK, head), f32),
            pltpu.VMEM((n_section, BLOCK, head), f32),
            pltpu.VMEM((n_section, BLOCK, head), f32),
            dma((5,)),
            dma((n_section,)),
            dma((n_section - 1,)),
            dma((n_section,)),
            dma((n_section - 1,)),
            dma((n_section,)),
            dma((n_section - 1,)),
            dma((n_section,)),
            dma((n_section - 1,)),
            dma((n_section,)),
            dma((n_section, n_section - 1)),
            dma((n_section, n_section)),
            dma((n_line - 1,)),
            dma((n_line, n_section - 1)),
            dma((n_line, n_section)),
            dma((n_blocks,)),
            dma((n_section, n_section - 1)),
            dma((n_section, n_section)),
        ],
        compiler_params=pltpu.CompilerParams(
            collective_id=0, has_side_effects=True, vmem_limit_bytes=60 * 1024 * 1024
        ),
    )(
        hidden,
        norm_gain,
        query_weight,
        key_weight,
        value_weight,
        block_reach,
        header_ids,
    )
    return jnp.dot(
        attended.reshape(rows, n_section * head), output_weight, preferred_element_type=f32
    ).astype(bf16)


def solution(mesh):
    n_section, n_seq = mesh.shape["section"], mesh.shape["seq"]
    if n_section * n_seq <= FUSED_BLOCKS:
        program = functools.partial(on_device_fused, n_section, n_seq)
    else:
        program = on_device
    return jax.shard_map(
        program,
        mesh=mesh,
        in_specs=(
            P("seq", "section"),
            P("section"),
            P(None, "section"),
            P("section", None),
            P("section", None),
            P(None, "section"),
            P("seq"),
            P(),
        ),
        out_specs=P("seq", "section"),
        check_vma=False,
    )
```

```python
import functools
import math

import jax
import jax.numpy as jnp
from jax import lax
from jax.experimental import pallas as pl
from jax.experimental.pallas import tpu as pltpu
from jax.sharding import PartitionSpec as P

BLOCK = 128
REACH = 2


EPSILON = 1e-05
THETA = 500000.0


def merged(value, axis, combine):
    everything = jax.tree.map(lambda part: lax.all_gather(part, axis), value)
    leading = jax.tree.map(lambda part: part[0], everything)

    def lap(k, so_far):
        return combine(so_far, jax.tree.map(lambda part: part[k], everything))

    return lax.fori_loop(1, lax.axis_size(axis), lap, leading)


def padded(cells, sides, width):
    for axis, dim in sides:
        count = lax.axis_size(axis)
        ends = count - 1
        head = lax.slice_in_dim(cells, 0, width, axis=dim)
        tail = lax.slice_in_dim(cells, cells.shape[dim] - width, cells.shape[dim], axis=dim)
        cells = jnp.concatenate(
            [
                lax.ppermute(tail, axis, [(i, (i + 1) % count) for i in range(ends)]),
                cells,
                lax.ppermute(head, axis, [((i + 1) % count, i) for i in range(ends)]),
            ],
            axis=dim,
        )
    return cells


def tables(positions, head_width):
    middle = head_width // 2
    frequency = jnp.exp(
        -(2.0 / head_width) * math.log(THETA) * jnp.arange(middle, dtype=jnp.float32)
    )
    angles = positions.astype(jnp.float32)[:, None] * frequency[None, :]
    angles = jnp.concatenate([angles, angles], axis=1)
    return (jnp.cos(angles), jnp.sin(angles))


def rotate(values, cosine_table, sine_table):
    middle = values.shape[-1] // 2
    turned = jnp.concatenate([-values[..., middle:], values[..., :middle]], axis=-1)
    return values * cosine_table + turned * sine_table


def combine_parts(earlier, later):
    first_max, first_total, first_out = earlier
    second_max, second_total, second_out = later
    overall = jnp.maximum(first_max, second_max)
    first_factor = jnp.exp(first_max - overall)
    second_factor = jnp.exp(second_max - overall)
    return (
        overall,
        first_total * first_factor + second_total * second_factor,
        first_out * first_factor[:, None] + second_out * second_factor[:, None],
    )


def on_device(
    hidden,
    norm_gain,
    query_weight,
    key_weight,
    value_weight,
    output_weight,
    block_reach,
    header_ids,
):
    row_count = hidden.shape[0]
    part_width = hidden.shape[1]
    head_width = key_weight.shape[1]
    local_blocks = row_count // BLOCK
    total_blocks = local_blocks * lax.axis_size("seq")
    seq_place = lax.axis_index("seq")
    floats = hidden.astype(jnp.float32)
    squares = lax.psum(jnp.sum(floats * floats, axis=1), "section")
    scaling = lax.rsqrt(squares / (part_width * lax.axis_size("section")) + EPSILON)
    normed_part = (floats * scaling[:, None] * norm_gain.astype(jnp.float32)[None, :]).astype(
        jnp.bfloat16
    )
    weight_rows = query_weight
    query_sum = jnp.dot(
        lax.all_gather(normed_part, "section", axis=1, tiled=True),
        weight_rows,
        preferred_element_type=jnp.float32,
    )
    key_sum, value_sum = lax.psum(
        (
            jnp.dot(normed_part, key_weight, preferred_element_type=jnp.float32),
            jnp.dot(normed_part, value_weight, preferred_element_type=jnp.float32),
        ),
        "section",
    )
    positions = seq_place * row_count + jnp.arange(row_count, dtype=jnp.int32)
    cosine_table, sine_table = tables(positions, head_width)
    queries = rotate(query_sum, cosine_table, sine_table).astype(jnp.bfloat16)
    keys_here = rotate(key_sum, cosine_table, sine_table).astype(jnp.bfloat16)
    values_here = value_sum.astype(jnp.bfloat16)
    packed = jnp.concatenate([queries, keys_here, values_here], axis=1)
    block_numbers = seq_place * local_blocks + jnp.arange(local_blocks, dtype=jnp.int32)
    select = header_ids[:, None] == block_numbers[None, :]
    shaped = packed.reshape(local_blocks, BLOCK, 3 * head_width)
    picked = jnp.einsum(
        "hb,bre->hre", select.astype(jnp.bfloat16), shaped, preferred_element_type=jnp.float32
    )
    header_pack = lax.psum(picked, "seq").astype(jnp.bfloat16).reshape(-1, 3 * head_width)
    head_queries = header_pack[:, :head_width]
    head_keys = header_pack[:, head_width : 2 * head_width]
    head_values = header_pack[:, 2 * head_width :]
    inverse_root = 1.0 / math.sqrt(head_width)
    far_scores = (
        jnp.einsum("qd,kd->qk", head_queries, keys_here, preferred_element_type=jnp.float32)
        * inverse_root
    )
    far_max = jnp.max(far_scores, axis=1)
    far_weights = jnp.exp(far_scores - far_max[:, None])
    far_total = jnp.sum(far_weights, axis=1)
    far_out = jnp.dot(
        far_weights.astype(jnp.bfloat16), values_here, preferred_element_type=jnp.float32
    )
    merged_max, merged_total, merged_out = merged(
        (far_max, far_total, far_out), "seq", combine_parts
    )
    header_result = merged_out / merged_total[:, None]
    margin_rows = REACH * BLOCK
    stacked = jnp.concatenate([keys_here, values_here], axis=1)
    extended = padded(stacked, (("seq", 0),), margin_rows)
    near_keys = extended[:, :head_width]
    near_values = extended[:, head_width:]
    extent = row_count + 2 * margin_rows
    key_blocks = seq_place * local_blocks - REACH + jnp.arange(extent, dtype=jnp.int32) // BLOCK
    query_blocks = seq_place * local_blocks + jnp.arange(row_count, dtype=jnp.int32) // BLOCK
    limits = jnp.repeat(block_reach, BLOCK)
    key_header = jnp.any(header_ids[:, None] == key_blocks[None, :], axis=0)
    allowed = (key_blocks >= 0)[None, :] & (key_blocks < total_blocks)[None, :]
    allowed = allowed & (jnp.abs(key_blocks[None, :] - query_blocks[:, None]) <= limits[:, None])
    allowed = allowed & jnp.logical_not(key_header)[None, :]
    near_scores = (
        jnp.einsum("qd,kd->qk", queries, near_keys, preferred_element_type=jnp.float32)
        * inverse_root
    )
    near_scores = jnp.where(allowed, near_scores, -jnp.inf)
    head_scores = (
        jnp.einsum("qd,kd->qk", queries, head_keys, preferred_element_type=jnp.float32)
        * inverse_root
    )
    scores = jnp.concatenate([near_scores, head_scores], axis=1)
    row_top = jnp.max(scores, axis=1)
    weights = jnp.exp(scores - row_top[:, None])
    row_sums = jnp.sum(weights, axis=1)
    joined = jnp.concatenate([near_values, head_values], axis=0)
    mixed_out = (
        jnp.dot(weights.astype(jnp.bfloat16), joined, preferred_element_type=jnp.float32)
        / row_sums[:, None]
    )
    header_local = jnp.einsum(
        "hb,hre->bre", select.astype(jnp.float32), header_result.reshape(-1, BLOCK, head_width)
    )
    is_local_header = jnp.any(select, axis=0)
    attended = jnp.where(
        is_local_header[:, None, None],
        header_local,
        mixed_out.reshape(local_blocks, BLOCK, head_width),
    )
    attended = attended.reshape(row_count, head_width).astype(jnp.bfloat16)
    weight_rows = output_weight
    result = jnp.dot(
        lax.all_gather(attended, "section", axis=1, tiled=True),
        weight_rows,
        preferred_element_type=jnp.float32,
    )
    return result.astype(jnp.bfloat16)


MESH = pl.DeviceIdType.MESH
LOW = -1e30
FUSED_BLOCKS = 64


def fused(
    n_section,
    n_line,
    hidden_ref,
    gain_ref,
    query_ref,
    key_ref,
    value_ref,
    reach_ref,
    ids_ref,
    out_ref,
    x,
    scaled,
    wq,
    wkv,
    squares,
    squares_got,
    kv_part,
    kv_got,
    q_part,
    q_got,
    blocks,
    queries,
    top,
    total,
    acc,
    local_sem,
    x_sem,
    w_send,
    w_recv,
    wf_send,
    wf_recv,
    sq_send,
    sq_recv,
    kv_send,
    kv_recv,
    q_send,
    q_recv,
    line_send,
    plane_send,
    twin_send,
    block_recv,
    out_send,
    out_recv,
):
    width = x.shape[1]
    half = width // 2
    head = wq.shape[2]
    s = lax.axis_index("section")
    j = lax.axis_index("seq")
    z = j // 2
    c = j % 2
    twin = z * 2 + (1 - c)
    others = [(s + k) % n_section for k in range(1, n_section)]
    line = [((z + k) % n_line) * 2 + c for k in range(1, n_line)]

    def push(src, dst, send, recv, section, seq):
        copy = pltpu.make_async_remote_copy(
            src_ref=src,
            dst_ref=dst,
            send_sem=send,
            recv_sem=recv,
            device_id=(section, seq),
            device_id_type=MESH,
        )
        copy.start()
        pending.append(copy)

    def arrived(dst, recv):
        pltpu.make_async_remote_copy(
            src_ref=dst,
            dst_ref=dst,
            send_sem=local_sem.at[4],
            recv_sem=recv,
            device_id=(s, twin),
            device_id_type=MESH,
        ).wait_recv()

    pending = []
    get_x = []
    for r in range(n_section):
        rows = pl.ds(r * BLOCK, BLOCK)
        get_x.append(pltpu.make_async_copy(hidden_ref.at[rows, :], x.at[rows, :], x_sem.at[r]))
        get_x[r].start()
    get_k = pltpu.make_async_copy(key_ref, wkv.at[:, 0:head], local_sem.at[1])
    get_v = pltpu.make_async_copy(value_ref, wkv.at[:, head : 2 * head], local_sem.at[2])
    get_q = pltpu.make_async_copy(
        query_ref.at[pl.ds(pl.multiple_of(s * width, width), width), :], wq.at[s], local_sem.at[3]
    )
    get_k.start()
    get_v.start()
    get_q.start()

    barrier = pltpu.get_barrier_semaphore()
    friends = [(t, j) for t in others] + [(s, i) for i in line] + [(s, twin)]
    for friend in friends:
        pl.semaphore_signal(barrier, inc=1, device_id=friend, device_id_type=MESH)

    gain = gain_ref[...].astype(jnp.float32).reshape(1, width)
    for r in range(n_section):
        get_x[r].wait()
        part = x[r * BLOCK : (r + 1) * BLOCK, :].astype(jnp.float32)
        scaled[r * BLOCK : (r + 1) * BLOCK, :] = (part * gain).astype(jnp.bfloat16)
    get_k.wait()
    get_v.wait()
    kv_part[...] = (
        jnp.dot(scaled[...], wkv[...], preferred_element_type=jnp.float32)
        .astype(jnp.bfloat16)
        .reshape(kv_part.shape)
    )
    pl.semaphore_wait(barrier, len(friends))
    for k, t in enumerate(others):
        push(kv_part.at[t], kv_got.at[s], kv_send.at[k], kv_recv.at[s], t, j)

    mine = pl.ds(pl.multiple_of(c * half, half), half)
    for k, t in enumerate(others):
        push(
            query_ref.at[pl.ds(pl.multiple_of(t * width + c * half, half), half), :],
            wq.at[s, mine, :],
            w_send.at[k],
            w_recv.at[s],
            t,
            j,
        )

    for r in range(n_section):
        part = x[r * BLOCK : (r + 1) * BLOCK, :].astype(jnp.float32)
        column = jnp.sum(part * part, axis=1, keepdims=True)
        squares[r] = jnp.transpose(jnp.broadcast_to(column, (BLOCK, BLOCK)))[:8, :]
    for k, t in enumerate(others):
        push(squares.at[t], squares_got.at[s], sq_send.at[k], sq_recv.at[s], t, j)

    b = j * n_section + s
    lanes = lax.broadcasted_iota(jnp.int32, (BLOCK, head), 1)
    positions = b * BLOCK + lax.broadcasted_iota(jnp.int32, (BLOCK, head), 0)
    spots = lax.rem(lanes, head // 2).astype(jnp.float32)
    angles = positions.astype(jnp.float32) * jnp.exp(-(2.0 / head) * math.log(THETA) * spots)
    cosine = jnp.cos(angles)
    sine = jnp.where(lanes < head // 2, -1.0, 1.0) * jnp.sin(angles)

    def project(k):
        owner = (s + k) % n_section
        q_part[k] = (
            jnp.dot(scaled[...], wq[owner], preferred_element_type=jnp.float32)
            .astype(jnp.bfloat16)
            .reshape(q_part.shape[1:])
        )
        for i, t in enumerate(others):
            push(q_part.at[k, t], q_got.at[s, owner], q_send.at[k, i], q_recv.at[s, owner], t, j)

    get_q.wait()
    project(0)

    def turned(values):
        return values * cosine + pltpu.roll(values, head // 2, axis=1) * sine

    for t in others:
        arrived(squares_got.at[t], sq_recv.at[t])
    sums = squares[s]
    for t in others:
        sums = sums + squares_got[t]
    scaling = lax.rsqrt(sums / (width * n_section) + EPSILON)
    scaling = jnp.transpose(jnp.broadcast_to(scaling[0:1, :], (BLOCK, BLOCK)))
    for t in others:
        arrived(kv_got.at[t], kv_recv.at[t])
    kv = kv_part[s].astype(jnp.float32)
    for t in others:
        kv = kv + kv_got[t].astype(jnp.float32)
    blocks[b, :, 0:head] = turned(kv[:, :head] * scaling).astype(jnp.bfloat16)
    blocks[b, :, head : 2 * head] = (kv[:, head:] * scaling).astype(jnp.bfloat16)

    across = s + 1 - 2 * (s % 2)
    along = (s + 2) % n_section
    corner = (across + 2) % n_section
    relayed = jnp.where(c == 0, across, along)
    direct = jnp.where(c == 0, along, across)

    def hand(number, send, section, seq):
        push(blocks.at[number], blocks.at[number], send, block_recv.at[number], section, seq)

    def spread(number, slot):
        hand(number, plane_send.at[slot, 0], relayed, j)
        hand(number, plane_send.at[slot, 1], direct, j)
        hand(number, twin_send.at[slot, 0], s, twin)

    for k, i in enumerate(line):
        push(blocks.at[b], blocks.at[b], line_send.at[k], block_recv.at[b], s, i)
    spread(b, 0)

    def relay(i, seq):
        number = seq * n_section + relayed
        arrived(blocks.at[number], block_recv.at[number])
        hand(number, plane_send.at[i, 2], direct, j)
        hand(number, twin_send.at[i, 1], s, twin)

    for k, i in enumerate(line):
        number = i * n_section + s
        arrived(blocks.at[number], block_recv.at[number])
        spread(number, k + 1)
    for k, t in enumerate(others):
        arrived(wq.at[t, mine, :], w_recv.at[t])
        push(wq.at[t, mine, :], wq.at[t, mine, :], wf_send.at[k], wf_recv.at[t], s, twin)
    relay(0, j)
    theirs = pl.ds(pl.multiple_of((1 - c) * half, half), half)
    for k, t in enumerate(others):
        arrived(wq.at[t, theirs, :], wf_recv.at[t])
        project(k + 1)
    for k, i in enumerate(line):
        relay(k + 1, i)

    for t in others:
        for h in range(n_section):
            arrived(q_got.at[t, h], q_recv.at[t, h])
    for h in range(n_section):
        place = (h + n_section - s) % n_section
        value = q_part[place, s].astype(jnp.float32)
        for t in others:
            value = value + q_got[t, h].astype(jnp.float32)
        queries[h] = turned(value * scaling).astype(jnp.bfloat16)

    first = ids_ref[0]
    second = ids_ref[1]
    own_header = jnp.logical_or(first == b, second == b)
    limit = jnp.where(own_header, n_section * n_line * 2, reach_ref[s])
    group = n_section * BLOCK
    factor = 1.4426950408889634 / math.sqrt(head)
    top[...] = jnp.full(top.shape, LOW, jnp.float32)
    total[...] = jnp.zeros(total.shape, jnp.float32)
    acc[...] = jnp.zeros(acc.shape, jnp.float32)

    def attend(seq):
        start = seq * n_section
        numbers = start + lax.broadcasted_iota(jnp.int32, (1, group), 1) // BLOCK
        valid = (numbers == first) | (numbers == second) | (jnp.abs(numbers - b) <= limit)
        bias = jnp.where(valid, 0.0, LOW)
        keys = blocks[pl.ds(start, n_section), :, 0:head].reshape(group, head)
        values = blocks[pl.ds(start, n_section), :, head : 2 * head].reshape(group, head)
        for h in range(n_section):
            scores = lax.dot_general(
                queries[h], keys, (((1,), (1,)), ((), ())), preferred_element_type=jnp.float32
            )
            scores = scores * factor + bias
            before = top[h]
            after = jnp.maximum(before, jnp.max(scores, axis=1, keepdims=True))
            fade = jnp.exp2(before - after)
            weights = jnp.exp2(scores - after[:, 0:1])
            top[h] = after
            total[h] = total[h] * fade + jnp.sum(weights, axis=1, keepdims=True)
            acc[h] = acc[h] * fade + jnp.dot(
                weights.astype(jnp.bfloat16), values, preferred_element_type=jnp.float32
            )

    def attend_twin(i):
        seq = ((z + i) % n_line) * 2 + (1 - c)
        for t in range(n_section):
            arrived(blocks.at[seq * n_section + t], block_recv.at[seq * n_section + t])
        attend(seq)

    for i in range(n_line):
        seq = ((z + i) % n_line) * 2 + c
        for k, t in enumerate([direct, corner]):
            number = seq * n_section + t
            arrived(blocks.at[number], block_recv.at[number])
            hand(number, twin_send.at[i, k + 2], s, twin)
        attend(seq)
        if i > 0:
            attend_twin(i - 1)
    attend_twin(n_line - 1)

    for h in range(n_section):
        columns = pl.ds(h * head, head)
        out_ref[s, :, columns] = (acc[h] / total[h]).astype(jnp.bfloat16)
        piece = out_ref.at[s, :, columns]
        for k, t in enumerate(others):
            push(piece, piece, out_send.at[h, k], out_recv.at[s, h], t, j)
    for t in others:
        for h in range(n_section):
            arrived(out_ref.at[t, :, pl.ds(h * head, head)], out_recv.at[t, h])
    for copy in pending:
        copy.wait_send()


def on_device_fused(
    n_section,
    n_seq,
    hidden,
    norm_gain,
    query_weight,
    key_weight,
    value_weight,
    output_weight,
    block_reach,
    header_ids,
):
    rows, width = hidden.shape
    head = key_weight.shape[1]
    n_line = n_seq // 2
    n_blocks = n_section * n_seq
    vmem = pl.BlockSpec(memory_space=pltpu.VMEM)
    smem = pl.BlockSpec(memory_space=pltpu.SMEM)
    anywhere = pl.BlockSpec(memory_space=pltpu.HBM)
    dma = pltpu.SemaphoreType.DMA
    bf16 = jnp.bfloat16
    f32 = jnp.float32
    attended = pl.pallas_call(
        functools.partial(fused, n_section, n_line),
        out_shape=jax.ShapeDtypeStruct((n_section, BLOCK, n_section * head), bf16),
        in_specs=[anywhere, vmem, anywhere, anywhere, anywhere, smem, smem],
        out_specs=vmem,
        scratch_shapes=[
            pltpu.VMEM((rows, width), bf16),
            pltpu.VMEM((rows, width), bf16),
            pltpu.VMEM((n_section, width, head), bf16),
            pltpu.VMEM((width, 2 * head), bf16),
            pltpu.VMEM((n_section, 8, BLOCK), f32),
            pltpu.VMEM((n_section, 8, BLOCK), f32),
            pltpu.VMEM((n_section, BLOCK, 2 * head), bf16),
            pltpu.VMEM((n_section, BLOCK, 2 * head), bf16),
            pltpu.VMEM((n_section, n_section, BLOCK, head), bf16),
            pltpu.VMEM((n_section, n_section, BLOCK, head), bf16),
            pltpu.VMEM((n_blocks, BLOCK, 2 * head), bf16),
            pltpu.VMEM((n_section, BLOCK, head), bf16),
            pltpu.VMEM((n_section, BLOCK, head), f32),
            pltpu.VMEM((n_section, BLOCK, head), f32),
            pltpu.VMEM((n_section, BLOCK, head), f32),
            dma((5,)),
            dma((n_section,)),
            dma((n_section - 1,)),
            dma((n_section,)),
            dma((n_section - 1,)),
            dma((n_section,)),
            dma((n_section - 1,)),
            dma((n_section,)),
            dma((n_section - 1,)),
            dma((n_section,)),
            dma((n_section, n_section - 1)),
            dma((n_section, n_section)),
            dma((n_line - 1,)),
            dma((n_line, n_section - 1)),
            dma((n_line, n_section)),
            dma((n_blocks,)),
            dma((n_section, n_section - 1)),
            dma((n_section, n_section)),
        ],
        compiler_params=pltpu.CompilerParams(
            collective_id=0, has_side_effects=True, vmem_limit_bytes=60 * 1024 * 1024
        ),
    )(
        hidden,
        norm_gain,
        query_weight,
        key_weight,
        value_weight,
        block_reach,
        header_ids,
    )
    return jnp.dot(
        attended.reshape(rows, n_section * head), output_weight, preferred_element_type=f32
    ).astype(bf16)


def solution(mesh):
    n_section, n_seq = mesh.shape["section"], mesh.shape["seq"]
    if n_section * n_seq <= FUSED_BLOCKS:
        program = functools.partial(on_device_fused, n_section, n_seq)
    else:
        program = on_device
    return jax.shard_map(
        program,
        mesh=mesh,
        in_specs=(
            P("seq", "section"),
            P("section"),
            P(None, "section"),
            P("section", None),
            P("section", None),
            P(None, "section"),
            P("seq"),
            P(),
        ),
        out_specs=P("seq", "section"),
        check_vma=False,
    )
```

```python
import functools
import math

import jax
import jax.numpy as jnp
from jax import lax
from jax.experimental import pallas as pl
from jax.experimental.pallas import tpu as pltpu
from jax.sharding import PartitionSpec as P

BLOCK = 128
REACH = 2


EPSILON = 1e-05
THETA = 500000.0


def merged(value, axis, combine):
    everything = jax.tree.map(lambda part: lax.all_gather(part, axis), value)
    leading = jax.tree.map(lambda part: part[0], everything)

    def lap(k, so_far):
        return combine(so_far, jax.tree.map(lambda part: part[k], everything))

    return lax.fori_loop(1, lax.axis_size(axis), lap, leading)


def padded(cells, sides, width):
    for axis, dim in sides:
        count = lax.axis_size(axis)
        ends = count - 1
        head = lax.slice_in_dim(cells, 0, width, axis=dim)
        tail = lax.slice_in_dim(cells, cells.shape[dim] - width, cells.shape[dim], axis=dim)
        cells = jnp.concatenate(
            [
                lax.ppermute(tail, axis, [(i, (i + 1) % count) for i in range(ends)]),
                cells,
                lax.ppermute(head, axis, [((i + 1) % count, i) for i in range(ends)]),
            ],
            axis=dim,
        )
    return cells


def tables(positions, head_width):
    middle = head_width // 2
    frequency = jnp.exp(
        -(2.0 / head_width) * math.log(THETA) * jnp.arange(middle, dtype=jnp.float32)
    )
    angles = positions.astype(jnp.float32)[:, None] * frequency[None, :]
    angles = jnp.concatenate([angles, angles], axis=1)
    return (jnp.cos(angles), jnp.sin(angles))


def rotate(values, cosine_table, sine_table):
    middle = values.shape[-1] // 2
    turned = jnp.concatenate([-values[..., middle:], values[..., :middle]], axis=-1)
    return values * cosine_table + turned * sine_table


def combine_parts(earlier, later):
    first_max, first_total, first_out = earlier
    second_max, second_total, second_out = later
    overall = jnp.maximum(first_max, second_max)
    first_factor = jnp.exp(first_max - overall)
    second_factor = jnp.exp(second_max - overall)
    return (
        overall,
        first_total * first_factor + second_total * second_factor,
        first_out * first_factor[:, None] + second_out * second_factor[:, None],
    )


def on_device(
    hidden,
    norm_gain,
    query_weight,
    key_weight,
    value_weight,
    output_weight,
    block_reach,
    header_ids,
):
    row_count = hidden.shape[0]
    part_width = hidden.shape[1]
    head_width = key_weight.shape[1]
    local_blocks = row_count // BLOCK
    total_blocks = local_blocks * lax.axis_size("seq")
    seq_place = lax.axis_index("seq")
    floats = hidden.astype(jnp.float32)
    squares = lax.psum(jnp.sum(floats * floats, axis=1), "section")
    scaling = lax.rsqrt(squares / (part_width * lax.axis_size("section")) + EPSILON)
    normed_part = (floats * scaling[:, None] * norm_gain.astype(jnp.float32)[None, :]).astype(
        jnp.bfloat16
    )
    weight_rows = query_weight
    query_sum = jnp.dot(
        lax.all_gather(normed_part, "section", axis=1, tiled=True),
        weight_rows,
        preferred_element_type=jnp.float32,
    )
    key_sum, value_sum = lax.psum(
        (
            jnp.dot(normed_part, key_weight, preferred_element_type=jnp.float32),
            jnp.dot(normed_part, value_weight, preferred_element_type=jnp.float32),
        ),
        "section",
    )
    positions = seq_place * row_count + jnp.arange(row_count, dtype=jnp.int32)
    cosine_table, sine_table = tables(positions, head_width)
    queries = rotate(query_sum, cosine_table, sine_table).astype(jnp.bfloat16)
    keys_here = rotate(key_sum, cosine_table, sine_table).astype(jnp.bfloat16)
    values_here = value_sum.astype(jnp.bfloat16)
    packed = jnp.concatenate([queries, keys_here, values_here], axis=1)
    block_numbers = seq_place * local_blocks + jnp.arange(local_blocks, dtype=jnp.int32)
    select = header_ids[:, None] == block_numbers[None, :]
    shaped = packed.reshape(local_blocks, BLOCK, 3 * head_width)
    picked = jnp.einsum(
        "hb,bre->hre", select.astype(jnp.bfloat16), shaped, preferred_element_type=jnp.float32
    )
    header_pack = lax.psum(picked, "seq").astype(jnp.bfloat16).reshape(-1, 3 * head_width)
    head_queries = header_pack[:, :head_width]
    head_keys = header_pack[:, head_width : 2 * head_width]
    head_values = header_pack[:, 2 * head_width :]
    inverse_root = 1.0 / math.sqrt(head_width)
    far_scores = (
        jnp.einsum("qd,kd->qk", head_queries, keys_here, preferred_element_type=jnp.float32)
        * inverse_root
    )
    far_max = jnp.max(far_scores, axis=1)
    far_weights = jnp.exp(far_scores - far_max[:, None])
    far_total = jnp.sum(far_weights, axis=1)
    far_out = jnp.dot(
        far_weights.astype(jnp.bfloat16), values_here, preferred_element_type=jnp.float32
    )
    merged_max, merged_total, merged_out = merged(
        (far_max, far_total, far_out), "seq", combine_parts
    )
    header_result = merged_out / merged_total[:, None]
    margin_rows = REACH * BLOCK
    stacked = jnp.concatenate([keys_here, values_here], axis=1)
    extended = padded(stacked, (("seq", 0),), margin_rows)
    near_keys = extended[:, :head_width]
    near_values = extended[:, head_width:]
    extent = row_count + 2 * margin_rows
    key_blocks = seq_place * local_blocks - REACH + jnp.arange(extent, dtype=jnp.int32) // BLOCK
    query_blocks = seq_place * local_blocks + jnp.arange(row_count, dtype=jnp.int32) // BLOCK
    limits = jnp.repeat(block_reach, BLOCK)
    key_header = jnp.any(header_ids[:, None] == key_blocks[None, :], axis=0)
    allowed = (key_blocks >= 0)[None, :] & (key_blocks < total_blocks)[None, :]
    allowed = allowed & (jnp.abs(key_blocks[None, :] - query_blocks[:, None]) <= limits[:, None])
    allowed = allowed & jnp.logical_not(key_header)[None, :]
    near_scores = (
        jnp.einsum("qd,kd->qk", queries, near_keys, preferred_element_type=jnp.float32)
        * inverse_root
    )
    near_scores = jnp.where(allowed, near_scores, -jnp.inf)
    head_scores = (
        jnp.einsum("qd,kd->qk", queries, head_keys, preferred_element_type=jnp.float32)
        * inverse_root
    )
    scores = jnp.concatenate([near_scores, head_scores], axis=1)
    row_top = jnp.max(scores, axis=1)
    weights = jnp.exp(scores - row_top[:, None])
    row_sums = jnp.sum(weights, axis=1)
    joined = jnp.concatenate([near_values, head_values], axis=0)
    mixed_out = (
        jnp.dot(weights.astype(jnp.bfloat16), joined, preferred_element_type=jnp.float32)
        / row_sums[:, None]
    )
    header_local = jnp.einsum(
        "hb,hre->bre", select.astype(jnp.float32), header_result.reshape(-1, BLOCK, head_width)
    )
    is_local_header = jnp.any(select, axis=0)
    attended = jnp.where(
        is_local_header[:, None, None],
        header_local,
        mixed_out.reshape(local_blocks, BLOCK, head_width),
    )
    attended = attended.reshape(row_count, head_width).astype(jnp.bfloat16)
    weight_rows = output_weight
    result = jnp.dot(
        lax.all_gather(attended, "section", axis=1, tiled=True),
        weight_rows,
        preferred_element_type=jnp.float32,
    )
    return result.astype(jnp.bfloat16)


MESH = pl.DeviceIdType.MESH
LOW = -1e30
FUSED_BLOCKS = 64


def fused(
    n_section,
    n_line,
    hidden_ref,
    gain_ref,
    query_ref,
    key_ref,
    value_ref,
    reach_ref,
    ids_ref,
    out_ref,
    x,
    scaled,
    wq,
    wkv,
    squares,
    squares_got,
    kv_part,
    kv_got,
    q_part,
    q_got,
    blocks,
    queries,
    top,
    fade,
    acc,
    scores,
    weights,
    local_sem,
    x_sem,
    w_send,
    w_recv,
    wz_send,
    wz_recv,
    wf_send,
    wf_recv,
    sq_send,
    sq_recv,
    kv_send,
    kv_recv,
    q_send,
    q_recv,
    line_send,
    plane_send,
    twin_send,
    block_recv,
    out_send,
    out_recv,
):
    width = x.shape[1]
    half = width // 2
    head = wq.shape[2]
    s = lax.axis_index("section")
    j = lax.axis_index("seq")
    z = j // 2
    c = j % 2
    twin = z * 2 + (1 - c)
    others = [(s + k) % n_section for k in range(1, n_section)]
    line = [((z + k) % n_line) * 2 + c for k in range(1, n_line)]

    def push(src, dst, send, recv, section, seq):
        copy = pltpu.make_async_remote_copy(
            src_ref=src,
            dst_ref=dst,
            send_sem=send,
            recv_sem=recv,
            device_id=(section, seq),
            device_id_type=MESH,
        )
        copy.start()
        pending.append(copy)

    def arrived(dst, recv):
        pltpu.make_async_remote_copy(
            src_ref=dst,
            dst_ref=dst,
            send_sem=local_sem.at[4],
            recv_sem=recv,
            device_id=(s, twin),
            device_id_type=MESH,
        ).wait_recv()

    pending = []
    get_x = []
    for r in range(n_section):
        rows = pl.ds(r * BLOCK, BLOCK)
        get_x.append(pltpu.make_async_copy(hidden_ref.at[rows, :], x.at[rows, :], x_sem.at[r]))
        get_x[r].start()
    get_k = pltpu.make_async_copy(key_ref, wkv.at[:, 0:head], local_sem.at[1])
    get_v = pltpu.make_async_copy(value_ref, wkv.at[:, head : 2 * head], local_sem.at[2])
    get_q = pltpu.make_async_copy(
        query_ref.at[pl.ds(pl.multiple_of(s * width, width), width), :], wq.at[s], local_sem.at[3]
    )
    get_k.start()
    get_v.start()
    get_q.start()

    barrier = pltpu.get_barrier_semaphore()
    friends = [(t, j) for t in others] + [(s, i) for i in line] + [(s, twin)]
    for friend in friends:
        pl.semaphore_signal(barrier, inc=1, device_id=friend, device_id_type=MESH)

    gain = gain_ref[...].astype(jnp.float32).reshape(1, width)
    for r in range(n_section):
        get_x[r].wait()
        part = x[r * BLOCK : (r + 1) * BLOCK, :].astype(jnp.float32)
        scaled[r * BLOCK : (r + 1) * BLOCK, :] = (part * gain).astype(jnp.bfloat16)
    get_k.wait()
    get_v.wait()
    kv_part[...] = (
        jnp.dot(scaled[...], wkv[...], preferred_element_type=jnp.float32)
        .astype(jnp.bfloat16)
        .reshape(kv_part.shape)
    )
    pl.semaphore_wait(barrier, len(friends))
    for k, t in enumerate(others):
        push(kv_part.at[t], kv_got.at[s], kv_send.at[k], kv_recv.at[s], t, j)

    quarter = half // 2
    partner = (z + 1 - 2 * (z % 2)) * 2 + c
    mine = pl.ds(pl.multiple_of(c * half, half), half)
    near = pl.ds(pl.multiple_of(c * half + (z % 2) * quarter, quarter), quarter)
    far = pl.ds(pl.multiple_of(c * half + (1 - z % 2) * quarter, quarter), quarter)
    for k, t in enumerate(others):
        push(
            query_ref.at[
                pl.ds(
                    pl.multiple_of(t * width + c * half + (z % 2) * quarter, quarter), quarter
                ),
                :,
            ],
            wq.at[s, near, :],
            w_send.at[k],
            w_recv.at[s],
            t,
            j,
        )

    for r in range(n_section):
        part = x[r * BLOCK : (r + 1) * BLOCK, :].astype(jnp.float32)
        column = jnp.sum(part * part, axis=1, keepdims=True)
        squares[r] = jnp.transpose(jnp.broadcast_to(column, (BLOCK, BLOCK)))[:8, :]
    for k, t in enumerate(others):
        push(squares.at[t], squares_got.at[s], sq_send.at[k], sq_recv.at[s], t, j)

    b = j * n_section + s
    lanes = lax.broadcasted_iota(jnp.int32, (BLOCK, head), 1)
    positions = b * BLOCK + lax.broadcasted_iota(jnp.int32, (BLOCK, head), 0)
    spots = lax.rem(lanes, head // 2).astype(jnp.float32)
    angles = positions.astype(jnp.float32) * jnp.exp(-(2.0 / head) * math.log(THETA) * spots)
    cosine = jnp.cos(angles)
    sine = jnp.where(lanes < head // 2, -1.0, 1.0) * jnp.sin(angles)

    def project(k):
        owner = (s + k) % n_section
        q_part[k] = (
            jnp.dot(scaled[...], wq[owner], preferred_element_type=jnp.float32)
            .astype(jnp.bfloat16)
            .reshape(q_part.shape[1:])
        )
        for i, t in enumerate(others):
            push(q_part.at[k, t], q_got.at[s, owner], q_send.at[k, i], q_recv.at[s, owner], t, j)

    get_q.wait()
    project(0)

    def turned(values):
        return values * cosine + pltpu.roll(values, head // 2, axis=1) * sine

    for t in others:
        arrived(squares_got.at[t], sq_recv.at[t])
    sums = squares[s]
    for t in others:
        sums = sums + squares_got[t]
    scaling = lax.rsqrt(sums / (width * n_section) + EPSILON)
    scaling = jnp.transpose(jnp.broadcast_to(scaling[0:1, :], (BLOCK, BLOCK)))
    for t in others:
        arrived(kv_got.at[t], kv_recv.at[t])
    kv = kv_part[s].astype(jnp.float32)
    for t in others:
        kv = kv + kv_got[t].astype(jnp.float32)
    blocks[b, :, 0:head] = jnp.transpose(turned(kv[:, :head] * scaling)).astype(jnp.bfloat16)
    blocks[b, :, head : 2 * head] = (kv[:, head:] * scaling).astype(jnp.bfloat16)

    across = s + 1 - 2 * (s % 2)
    along = (s + 2) % n_section
    corner = (across + 2) % n_section
    relayed = jnp.where(c == 0, across, along)
    direct = jnp.where(c == 0, along, across)

    def hand(number, send, section, seq):
        push(blocks.at[number], blocks.at[number], send, block_recv.at[number], section, seq)

    def spread(number, slot):
        hand(number, plane_send.at[slot, 0], relayed, j)
        hand(number, plane_send.at[slot, 1], direct, j)
        hand(number, twin_send.at[slot, 0], s, twin)

    for k, i in enumerate(line):
        push(blocks.at[b], blocks.at[b], line_send.at[k], block_recv.at[b], s, i)
    spread(b, 0)

    def relay(i, seq):
        number = seq * n_section + relayed
        arrived(blocks.at[number], block_recv.at[number])
        hand(number, plane_send.at[i, 2], direct, j)
        hand(number, twin_send.at[i, 1], s, twin)

    for k, t in enumerate(others):
        arrived(wq.at[t, near, :], w_recv.at[t])
        push(wq.at[t, near, :], wq.at[t, near, :], wz_send.at[k], wz_recv.at[t], s, partner)
    for k, i in enumerate(line):
        number = i * n_section + s
        arrived(blocks.at[number], block_recv.at[number])
        spread(number, k + 1)
    for k, t in enumerate(others):
        arrived(wq.at[t, far, :], wz_recv.at[t])
        push(wq.at[t, mine, :], wq.at[t, mine, :], wf_send.at[k], wf_recv.at[t], s, twin)
    relay(0, j)
    theirs = pl.ds(pl.multiple_of((1 - c) * half, half), half)
    for k, t in enumerate(others):
        arrived(wq.at[t, theirs, :], wf_recv.at[t])
        project(k + 1)
    for k, i in enumerate(line):
        relay(k + 1, i)

    for t in others:
        for h in range(n_section):
            arrived(q_got.at[t, h], q_recv.at[t, h])
    for h in range(n_section):
        place = (h + n_section - s) % n_section
        value = q_part[place, s].astype(jnp.float32)
        for t in others:
            value = value + q_got[t, h].astype(jnp.float32)
        queries[h * BLOCK : (h + 1) * BLOCK, :] = turned(value * scaling).astype(jnp.bfloat16)

    first = ids_ref[0]
    second = ids_ref[1]
    own_header = jnp.logical_or(first == b, second == b)
    limit = jnp.where(own_header, n_section * n_line * 2, reach_ref[s])
    group = 2 * n_section
    keys_wide = group * BLOCK
    factor = 1.4426950408889634 / math.sqrt(head)
    top[...] = jnp.full(top.shape, LOW, jnp.float32)
    acc[...] = jnp.zeros(acc.shape, jnp.float32)
    ones = jnp.ones((keys_wide, head), jnp.bfloat16)
    strip = 32

    def attend(place):
        start = place * group
        numbers = start + lax.broadcasted_iota(jnp.int32, (1, keys_wide), 1) // BLOCK
        valid = (numbers == first) | (numbers == second) | (jnp.abs(numbers - b) <= limit)
        bias = jnp.where(valid, 0.0, LOW)
        keys = jnp.concatenate([blocks[start + n, :, 0:head] for n in range(group)], axis=1)
        scores[...] = jnp.dot(queries[...], keys, preferred_element_type=jnp.float32)
        for r in range(0, n_section * BLOCK, strip):
            rows = pl.ds(r, strip)
            part = scores[rows, :] * factor + bias
            before = top[rows, :]
            after = jnp.maximum(before, jnp.max(part, axis=1, keepdims=True))
            weights[rows, :] = jnp.exp2(part - after[:, 0:1]).astype(jnp.bfloat16)
            fade[rows, :] = jnp.exp2(before - after)
            top[rows, :] = after
        values = blocks[pl.ds(start, group), :, head : 2 * head].reshape(keys_wide, head)
        gained = jnp.dot(
            weights[...],
            jnp.concatenate([values, ones], axis=1),
            preferred_element_type=jnp.float32,
        )
        factors = fade[...]
        acc[:, 0:head] = acc[:, 0:head] * factors + gained[:, 0:head]
        acc[:, head : 2 * head] = acc[:, head : 2 * head] * factors + gained[:, head : 2 * head]

    def pass_on(i):
        seq = ((z + i) % n_line) * 2 + c
        for k, t in enumerate([direct, corner]):
            number = seq * n_section + t
            arrived(blocks.at[number], block_recv.at[number])
            hand(number, twin_send.at[i, k + 2], s, twin)

    pass_on(0)
    for i in range(n_line):
        if i + 1 < n_line:
            pass_on(i + 1)
        place = (z + i) % n_line
        for t in range(n_section):
            number = (place * 2 + 1 - c) * n_section + t
            arrived(blocks.at[number], block_recv.at[number])
        attend(place)

    for h in range(n_section):
        columns = pl.ds(h * head, head)
        out_ref[s, :, columns] = (
            acc[h * BLOCK : (h + 1) * BLOCK, 0:head] / acc[h * BLOCK : (h + 1) * BLOCK, head : 2 * head]
        ).astype(jnp.bfloat16)
        piece = out_ref.at[s, :, columns]
        for k, t in enumerate(others):
            push(piece, piece, out_send.at[h, k], out_recv.at[s, h], t, j)
    for t in others:
        for h in range(n_section):
            arrived(out_ref.at[t, :, pl.ds(h * head, head)], out_recv.at[t, h])
    for copy in pending:
        copy.wait_send()


def on_device_fused(
    n_section,
    n_seq,
    hidden,
    norm_gain,
    query_weight,
    key_weight,
    value_weight,
    output_weight,
    block_reach,
    header_ids,
):
    rows, width = hidden.shape
    head = key_weight.shape[1]
    n_line = n_seq // 2
    n_blocks = n_section * n_seq
    vmem = pl.BlockSpec(memory_space=pltpu.VMEM)
    smem = pl.BlockSpec(memory_space=pltpu.SMEM)
    anywhere = pl.BlockSpec(memory_space=pltpu.HBM)
    dma = pltpu.SemaphoreType.DMA
    bf16 = jnp.bfloat16
    f32 = jnp.float32
    attended = pl.pallas_call(
        functools.partial(fused, n_section, n_line),
        out_shape=jax.ShapeDtypeStruct((n_section, BLOCK, n_section * head), bf16),
        in_specs=[anywhere, vmem, anywhere, anywhere, anywhere, smem, smem],
        out_specs=vmem,
        scratch_shapes=[
            pltpu.VMEM((rows, width), bf16),
            pltpu.VMEM((rows, width), bf16),
            pltpu.VMEM((n_section, width, head), bf16),
            pltpu.VMEM((width, 2 * head), bf16),
            pltpu.VMEM((n_section, 8, BLOCK), f32),
            pltpu.VMEM((n_section, 8, BLOCK), f32),
            pltpu.VMEM((n_section, BLOCK, 2 * head), bf16),
            pltpu.VMEM((n_section, BLOCK, 2 * head), bf16),
            pltpu.VMEM((n_section, n_section, BLOCK, head), bf16),
            pltpu.VMEM((n_section, n_section, BLOCK, head), bf16),
            pltpu.VMEM((n_blocks, BLOCK, 2 * head), bf16),
            pltpu.VMEM((n_section * BLOCK, head), bf16),
            pltpu.VMEM((n_section * BLOCK, head), f32),
            pltpu.VMEM((n_section * BLOCK, head), f32),
            pltpu.VMEM((n_section * BLOCK, 2 * head), f32),
            pltpu.VMEM((n_section * BLOCK, 2 * n_section * BLOCK), f32),
            pltpu.VMEM((n_section * BLOCK, 2 * n_section * BLOCK), bf16),
            dma((5,)),
            dma((n_section,)),
            dma((n_section - 1,)),
            dma((n_section,)),
            dma((n_section - 1,)),
            dma((n_section,)),
            dma((n_section - 1,)),
            dma((n_section,)),
            dma((n_section - 1,)),
            dma((n_section,)),
            dma((n_section - 1,)),
            dma((n_section,)),
            dma((n_section, n_section - 1)),
            dma((n_section, n_section)),
            dma((n_line - 1,)),
            dma((n_line, n_section - 1)),
            dma((n_line, n_section)),
            dma((n_blocks,)),
            dma((n_section, n_section - 1)),
            dma((n_section, n_section)),
        ],
        compiler_params=pltpu.CompilerParams(
            collective_id=0, has_side_effects=True, vmem_limit_bytes=60 * 1024 * 1024
        ),
    )(
        hidden,
        norm_gain,
        query_weight,
        key_weight,
        value_weight,
        block_reach,
        header_ids,
    )
    return jnp.dot(
        attended.reshape(rows, n_section * head), output_weight, preferred_element_type=f32
    ).astype(bf16)


def solution(mesh):
    n_section, n_seq = mesh.shape["section"], mesh.shape["seq"]
    if n_section * n_seq <= FUSED_BLOCKS:
        program = functools.partial(on_device_fused, n_section, n_seq)
    else:
        program = on_device
    return jax.shard_map(
        program,
        mesh=mesh,
        in_specs=(
            P("seq", "section"),
            P("section"),
            P(None, "section"),
            P("section", None),
            P("section", None),
            P(None, "section"),
            P("seq"),
            P(),
        ),
        out_specs=P("seq", "section"),
        check_vma=False,
    )
```

```python
import functools
import math

import jax
import jax.numpy as jnp
from jax import lax
from jax.experimental import pallas as pl
from jax.experimental.pallas import tpu as pltpu
from jax.sharding import PartitionSpec as P

BLOCK = 128
REACH = 2


EPSILON = 1e-05
THETA = 500000.0


def merged(value, axis, combine):
    everything = jax.tree.map(lambda part: lax.all_gather(part, axis), value)
    leading = jax.tree.map(lambda part: part[0], everything)

    def lap(k, so_far):
        return combine(so_far, jax.tree.map(lambda part: part[k], everything))

    return lax.fori_loop(1, lax.axis_size(axis), lap, leading)


def padded(cells, sides, width):
    for axis, dim in sides:
        count = lax.axis_size(axis)
        ends = count - 1
        head = lax.slice_in_dim(cells, 0, width, axis=dim)
        tail = lax.slice_in_dim(cells, cells.shape[dim] - width, cells.shape[dim], axis=dim)
        cells = jnp.concatenate(
            [
                lax.ppermute(tail, axis, [(i, (i + 1) % count) for i in range(ends)]),
                cells,
                lax.ppermute(head, axis, [((i + 1) % count, i) for i in range(ends)]),
            ],
            axis=dim,
        )
    return cells


def tables(positions, head_width):
    middle = head_width // 2
    frequency = jnp.exp(
        -(2.0 / head_width) * math.log(THETA) * jnp.arange(middle, dtype=jnp.float32)
    )
    angles = positions.astype(jnp.float32)[:, None] * frequency[None, :]
    angles = jnp.concatenate([angles, angles], axis=1)
    return (jnp.cos(angles), jnp.sin(angles))


def rotate(values, cosine_table, sine_table):
    middle = values.shape[-1] // 2
    turned = jnp.concatenate([-values[..., middle:], values[..., :middle]], axis=-1)
    return values * cosine_table + turned * sine_table


def combine_parts(earlier, later):
    first_max, first_total, first_out = earlier
    second_max, second_total, second_out = later
    overall = jnp.maximum(first_max, second_max)
    first_factor = jnp.exp(first_max - overall)
    second_factor = jnp.exp(second_max - overall)
    return (
        overall,
        first_total * first_factor + second_total * second_factor,
        first_out * first_factor[:, None] + second_out * second_factor[:, None],
    )


def on_device(
    hidden,
    norm_gain,
    query_weight,
    key_weight,
    value_weight,
    output_weight,
    block_reach,
    header_ids,
):
    row_count = hidden.shape[0]
    part_width = hidden.shape[1]
    head_width = key_weight.shape[1]
    local_blocks = row_count // BLOCK
    total_blocks = local_blocks * lax.axis_size("seq")
    seq_place = lax.axis_index("seq")
    floats = hidden.astype(jnp.float32)
    squares = lax.psum(jnp.sum(floats * floats, axis=1), "section")
    scaling = lax.rsqrt(squares / (part_width * lax.axis_size("section")) + EPSILON)
    normed_part = (floats * scaling[:, None] * norm_gain.astype(jnp.float32)[None, :]).astype(
        jnp.bfloat16
    )
    weight_rows = query_weight
    query_sum = jnp.dot(
        lax.all_gather(normed_part, "section", axis=1, tiled=True),
        weight_rows,
        preferred_element_type=jnp.float32,
    )
    key_sum, value_sum = lax.psum(
        (
            jnp.dot(normed_part, key_weight, preferred_element_type=jnp.float32),
            jnp.dot(normed_part, value_weight, preferred_element_type=jnp.float32),
        ),
        "section",
    )
    positions = seq_place * row_count + jnp.arange(row_count, dtype=jnp.int32)
    cosine_table, sine_table = tables(positions, head_width)
    queries = rotate(query_sum, cosine_table, sine_table).astype(jnp.bfloat16)
    keys_here = rotate(key_sum, cosine_table, sine_table).astype(jnp.bfloat16)
    values_here = value_sum.astype(jnp.bfloat16)
    packed = jnp.concatenate([queries, keys_here, values_here], axis=1)
    block_numbers = seq_place * local_blocks + jnp.arange(local_blocks, dtype=jnp.int32)
    select = header_ids[:, None] == block_numbers[None, :]
    shaped = packed.reshape(local_blocks, BLOCK, 3 * head_width)
    picked = jnp.einsum(
        "hb,bre->hre", select.astype(jnp.bfloat16), shaped, preferred_element_type=jnp.float32
    )
    header_pack = lax.psum(picked, "seq").astype(jnp.bfloat16).reshape(-1, 3 * head_width)
    head_queries = header_pack[:, :head_width]
    head_keys = header_pack[:, head_width : 2 * head_width]
    head_values = header_pack[:, 2 * head_width :]
    inverse_root = 1.0 / math.sqrt(head_width)
    far_scores = (
        jnp.einsum("qd,kd->qk", head_queries, keys_here, preferred_element_type=jnp.float32)
        * inverse_root
    )
    far_max = jnp.max(far_scores, axis=1)
    far_weights = jnp.exp(far_scores - far_max[:, None])
    far_total = jnp.sum(far_weights, axis=1)
    far_out = jnp.dot(
        far_weights.astype(jnp.bfloat16), values_here, preferred_element_type=jnp.float32
    )
    merged_max, merged_total, merged_out = merged(
        (far_max, far_total, far_out), "seq", combine_parts
    )
    header_result = merged_out / merged_total[:, None]
    margin_rows = REACH * BLOCK
    stacked = jnp.concatenate([keys_here, values_here], axis=1)
    extended = padded(stacked, (("seq", 0),), margin_rows)
    near_keys = extended[:, :head_width]
    near_values = extended[:, head_width:]
    extent = row_count + 2 * margin_rows
    key_blocks = seq_place * local_blocks - REACH + jnp.arange(extent, dtype=jnp.int32) // BLOCK
    query_blocks = seq_place * local_blocks + jnp.arange(row_count, dtype=jnp.int32) // BLOCK
    limits = jnp.repeat(block_reach, BLOCK)
    key_header = jnp.any(header_ids[:, None] == key_blocks[None, :], axis=0)
    allowed = (key_blocks >= 0)[None, :] & (key_blocks < total_blocks)[None, :]
    allowed = allowed & (jnp.abs(key_blocks[None, :] - query_blocks[:, None]) <= limits[:, None])
    allowed = allowed & jnp.logical_not(key_header)[None, :]
    near_scores = (
        jnp.einsum("qd,kd->qk", queries, near_keys, preferred_element_type=jnp.float32)
        * inverse_root
    )
    near_scores = jnp.where(allowed, near_scores, -jnp.inf)
    head_scores = (
        jnp.einsum("qd,kd->qk", queries, head_keys, preferred_element_type=jnp.float32)
        * inverse_root
    )
    scores = jnp.concatenate([near_scores, head_scores], axis=1)
    row_top = jnp.max(scores, axis=1)
    weights = jnp.exp(scores - row_top[:, None])
    row_sums = jnp.sum(weights, axis=1)
    joined = jnp.concatenate([near_values, head_values], axis=0)
    mixed_out = (
        jnp.dot(weights.astype(jnp.bfloat16), joined, preferred_element_type=jnp.float32)
        / row_sums[:, None]
    )
    header_local = jnp.einsum(
        "hb,hre->bre", select.astype(jnp.float32), header_result.reshape(-1, BLOCK, head_width)
    )
    is_local_header = jnp.any(select, axis=0)
    attended = jnp.where(
        is_local_header[:, None, None],
        header_local,
        mixed_out.reshape(local_blocks, BLOCK, head_width),
    )
    attended = attended.reshape(row_count, head_width).astype(jnp.bfloat16)
    weight_rows = output_weight
    result = jnp.dot(
        lax.all_gather(attended, "section", axis=1, tiled=True),
        weight_rows,
        preferred_element_type=jnp.float32,
    )
    return result.astype(jnp.bfloat16)


MESH = pl.DeviceIdType.MESH
LOW = -1e30
FUSED_BLOCKS = 64


def fused(
    n_section,
    n_line,
    hidden_ref,
    gain_ref,
    query_ref,
    key_ref,
    value_ref,
    reach_ref,
    ids_ref,
    out_ref,
    x,
    scaled,
    wq,
    wkv,
    squares,
    squares_got,
    kv_part,
    kv_got,
    q_part,
    q_got,
    key_blocks,
    value_blocks,
    queries,
    top,
    fade,
    acc,
    scores,
    weights,
    local_sem,
    x_sem,
    w_send,
    w_recv,
    wz_send,
    wz_recv,
    wf_send,
    wf_recv,
    sq_send,
    sq_recv,
    kv_send,
    kv_recv,
    q_send,
    q_recv,
    line_send,
    plane_send,
    twin_send,
    key_recv,
    value_plane_send,
    value_line_send,
    value_twin_send,
    value_recv,
    out_send,
    out_recv,
):
    width = x.shape[1]
    half = width // 2
    head = wq.shape[2]
    s = lax.axis_index("section")
    j = lax.axis_index("seq")
    z = j // 2
    c = j % 2
    twin = z * 2 + (1 - c)
    others = [(s + k) % n_section for k in range(1, n_section)]
    line = [((z + k) % n_line) * 2 + c for k in range(1, n_line)]

    def push(src, dst, send, recv, section, seq):
        copy = pltpu.make_async_remote_copy(
            src_ref=src,
            dst_ref=dst,
            send_sem=send,
            recv_sem=recv,
            device_id=(section, seq),
            device_id_type=MESH,
        )
        copy.start()
        pending.append(copy)

    def arrived(dst, recv):
        pltpu.make_async_remote_copy(
            src_ref=dst,
            dst_ref=dst,
            send_sem=local_sem.at[4],
            recv_sem=recv,
            device_id=(s, twin),
            device_id_type=MESH,
        ).wait_recv()

    pending = []
    get_x = []
    for r in range(n_section):
        rows = pl.ds(r * BLOCK, BLOCK)
        get_x.append(pltpu.make_async_copy(hidden_ref.at[rows, :], x.at[rows, :], x_sem.at[r]))
        get_x[r].start()
    get_k = pltpu.make_async_copy(key_ref, wkv.at[:, 0:head], local_sem.at[1])
    get_v = pltpu.make_async_copy(value_ref, wkv.at[:, head : 2 * head], local_sem.at[2])
    get_q = pltpu.make_async_copy(
        query_ref.at[pl.ds(pl.multiple_of(s * width, width), width), :], wq.at[s], local_sem.at[3]
    )
    get_k.start()
    get_v.start()
    get_q.start()

    barrier = pltpu.get_barrier_semaphore()
    friends = [(t, j) for t in others] + [(s, i) for i in line] + [(s, twin)]
    for friend in friends:
        pl.semaphore_signal(barrier, inc=1, device_id=friend, device_id_type=MESH)

    pl.semaphore_wait(barrier, len(friends))

    quarter = half // 2
    partner = (z + 1 - 2 * (z % 2)) * 2 + c
    mine = pl.ds(pl.multiple_of(c * half, half), half)
    near = pl.ds(pl.multiple_of(c * half + (z % 2) * quarter, quarter), quarter)
    far = pl.ds(pl.multiple_of(c * half + (1 - z % 2) * quarter, quarter), quarter)
    for k, t in enumerate(others):
        push(
            query_ref.at[
                pl.ds(
                    pl.multiple_of(t * width + c * half + (z % 2) * quarter, quarter), quarter
                ),
                :,
            ],
            wq.at[s, near, :],
            w_send.at[k],
            w_recv.at[s],
            t,
            j,
        )

    gain = gain_ref[...].astype(jnp.float32).reshape(1, width)
    for r in range(n_section):
        get_x[r].wait()
        part = x[r * BLOCK : (r + 1) * BLOCK, :].astype(jnp.float32)
        scaled[r * BLOCK : (r + 1) * BLOCK, :] = (part * gain).astype(jnp.bfloat16)
    get_k.wait()
    get_v.wait()
    kv_part[...] = (
        jnp.dot(scaled[...], wkv[...], preferred_element_type=jnp.float32)
        .astype(jnp.bfloat16)
        .reshape(kv_part.shape)
    )
    for k, t in enumerate(others):
        push(kv_part.at[t], kv_got.at[s], kv_send.at[k], kv_recv.at[s], t, j)

    for r in range(n_section):
        part = x[r * BLOCK : (r + 1) * BLOCK, :].astype(jnp.float32)
        column = jnp.sum(part * part, axis=1, keepdims=True)
        squares[r] = jnp.transpose(jnp.broadcast_to(column, (BLOCK, BLOCK)))[:8, :]
    for k, t in enumerate(others):
        push(squares.at[t], squares_got.at[s], sq_send.at[k], sq_recv.at[s], t, j)

    b = j * n_section + s
    lanes = lax.broadcasted_iota(jnp.int32, (BLOCK, head), 1)
    positions = b * BLOCK + lax.broadcasted_iota(jnp.int32, (BLOCK, head), 0)
    spots = lax.rem(lanes, head // 2).astype(jnp.float32)
    angles = positions.astype(jnp.float32) * jnp.exp(-(2.0 / head) * math.log(THETA) * spots)
    cosine = jnp.cos(angles)
    sine = jnp.where(lanes < head // 2, -1.0, 1.0) * jnp.sin(angles)

    def project(k):
        owner = (s + k) % n_section
        q_part[k] = (
            jnp.dot(scaled[...], wq[owner], preferred_element_type=jnp.float32)
            .astype(jnp.bfloat16)
            .reshape(q_part.shape[1:])
        )
        for i, t in enumerate(others):
            push(q_part.at[k, t], q_got.at[s, owner], q_send.at[k, i], q_recv.at[s, owner], t, j)

    get_q.wait()
    project(0)
    for k, t in enumerate(others):
        arrived(wq.at[t, near, :], w_recv.at[t])
        push(wq.at[t, near, :], wq.at[t, near, :], wz_send.at[k], wz_recv.at[t], s, partner)

    def turned(values):
        return values * cosine + pltpu.roll(values, head // 2, axis=1) * sine

    for t in others:
        arrived(squares_got.at[t], sq_recv.at[t])
    sums = squares[s]
    for t in others:
        sums = sums + squares_got[t]
    scaling = lax.rsqrt(sums / (width * n_section) + EPSILON)
    scaling = jnp.transpose(jnp.broadcast_to(scaling[0:1, :], (BLOCK, BLOCK)))
    for t in others:
        arrived(kv_got.at[t], kv_recv.at[t])
    kv = kv_part[s].astype(jnp.float32)
    for t in others:
        kv = kv + kv_got[t].astype(jnp.float32)
    key_blocks[b] = jnp.transpose(turned(kv[:, :head] * scaling)).astype(jnp.bfloat16)
    value_blocks[b] = (kv[:, head:] * scaling).astype(jnp.bfloat16)

    across = s + 1 - 2 * (s % 2)
    along = (s + 2) % n_section
    corner = (across + 2) % n_section
    relayed = jnp.where(c == 0, across, along)
    direct = jnp.where(c == 0, along, across)

    def hand_key(number, send, section, seq):
        piece = key_blocks.at[number]
        push(piece, piece, send, key_recv.at[number], section, seq)

    def hand_value(number, send, section, seq):
        piece = value_blocks.at[number]
        push(piece, piece, send, value_recv.at[number], section, seq)

    def await_key(number):
        arrived(key_blocks.at[number], key_recv.at[number])

    def await_value(number):
        arrived(value_blocks.at[number], value_recv.at[number])

    def spread_key(number, slot):
        hand_key(number, plane_send.at[slot, 0], relayed, j)
        hand_key(number, plane_send.at[slot, 1], direct, j)
        hand_key(number, twin_send.at[slot, 0], s, twin)

    def relay_key(slot, seq):
        number = seq * n_section + relayed
        await_key(number)
        hand_key(number, plane_send.at[slot, 2], direct, j)
        hand_key(number, twin_send.at[slot, 1], s, twin)

    def spread_value(number, slot):
        hand_value(number, value_twin_send.at[0, slot], s, twin)
        for k, i in enumerate(line):
            hand_value(number, value_line_send.at[slot, k], s, i)

    for k, i in enumerate(line):
        hand_key(b, line_send.at[k], s, i)
    hand_value(b, value_plane_send.at[0], relayed, j)
    hand_value(b, value_plane_send.at[1], direct, j)
    spread_key(b, 0)
    spread_value(b, 0)

    number = j * n_section + relayed
    await_value(number)
    hand_value(number, value_plane_send.at[2], direct, j)
    spread_value(number, 1)
    for k, t in enumerate(others):
        arrived(wq.at[t, far, :], wz_recv.at[t])
        push(wq.at[t, mine, :], wq.at[t, mine, :], wf_send.at[k], wf_recv.at[t], s, twin)
    for k, i in enumerate(line):
        number = i * n_section + s
        await_key(number)
        spread_key(number, k + 1)
    number = j * n_section + direct
    await_value(number)
    spread_value(number, 2)
    theirs = pl.ds(pl.multiple_of((1 - c) * half, half), half)
    for k, t in enumerate(others):
        arrived(wq.at[t, theirs, :], wf_recv.at[t])
        project(k + 1)
    relay_key(0, j)
    number = j * n_section + corner
    await_value(number)
    spread_value(number, 3)
    for k, i in enumerate(line):
        relay_key(k + 1, i)

    for t in others:
        for h in range(n_section):
            arrived(q_got.at[t, h], q_recv.at[t, h])
    for h in range(n_section):
        place = (h + n_section - s) % n_section
        value = q_part[place, s].astype(jnp.float32)
        for t in others:
            value = value + q_got[t, h].astype(jnp.float32)
        queries[h * BLOCK : (h + 1) * BLOCK, :] = turned(value * scaling).astype(jnp.bfloat16)

    first = ids_ref[0]
    second = ids_ref[1]
    own_header = jnp.logical_or(first == b, second == b)
    limit = jnp.where(own_header, n_section * n_line * 2, reach_ref[s])
    group = 2 * n_section
    keys_wide = group * BLOCK
    factor = 1.4426950408889634 / math.sqrt(head)
    top[...] = jnp.full(top.shape, LOW, jnp.float32)
    acc[...] = jnp.zeros(acc.shape, jnp.float32)
    ones = jnp.ones((keys_wide, head), jnp.bfloat16)
    strip = 32

    def attend(place):
        start = place * group
        numbers = start + lax.broadcasted_iota(jnp.int32, (1, keys_wide), 1) // BLOCK
        valid = (numbers == first) | (numbers == second) | (jnp.abs(numbers - b) <= limit)
        bias = jnp.where(valid, 0.0, LOW)
        keys = jnp.concatenate([key_blocks[start + n] for n in range(group)], axis=1)
        scores[...] = jnp.dot(queries[...], keys, preferred_element_type=jnp.float32)
        for r in range(0, n_section * BLOCK, strip):
            rows = pl.ds(r, strip)
            part = scores[rows, :] * factor + bias
            before = top[rows, :]
            after = jnp.maximum(before, jnp.max(part, axis=1, keepdims=True))
            weights[rows, :] = jnp.exp2(part - after[:, 0:1]).astype(jnp.bfloat16)
            fade[rows, :] = jnp.exp2(before - after)
            top[rows, :] = after
        values = value_blocks[pl.ds(start, group)].reshape(keys_wide, head)
        gained = jnp.dot(
            weights[...],
            jnp.concatenate([values, ones], axis=1),
            preferred_element_type=jnp.float32,
        )
        factors = fade[...]
        acc[:, 0:head] = acc[:, 0:head] * factors + gained[:, 0:head]
        acc[:, head : 2 * head] = acc[:, head : 2 * head] * factors + gained[:, head : 2 * head]

    def pass_on(i):
        seq = ((z + i) % n_line) * 2 + c
        for k, t in enumerate([direct, corner]):
            number = seq * n_section + t
            await_key(number)
            hand_key(number, twin_send.at[i, k + 2], s, twin)
        if i > 0:
            for t in range(n_section):
                number = seq * n_section + t
                await_value(number)
                hand_value(number, value_twin_send.at[i, t], s, twin)

    pass_on(0)
    for i in range(n_line):
        if i + 1 < n_line:
            pass_on(i + 1)
        place = (z + i) % n_line
        for t in range(n_section):
            number = (place * 2 + 1 - c) * n_section + t
            await_key(number)
            await_value(number)
        attend(place)

    for h in range(n_section):
        columns = pl.ds(h * head, head)
        out_ref[s, :, columns] = (
            acc[h * BLOCK : (h + 1) * BLOCK, 0:head] / acc[h * BLOCK : (h + 1) * BLOCK, head : 2 * head]
        ).astype(jnp.bfloat16)
        piece = out_ref.at[s, :, columns]
        for k, t in enumerate(others):
            push(piece, piece, out_send.at[h, k], out_recv.at[s, h], t, j)
    for t in others:
        for h in range(n_section):
            arrived(out_ref.at[t, :, pl.ds(h * head, head)], out_recv.at[t, h])
    for copy in pending:
        copy.wait_send()


def on_device_fused(
    n_section,
    n_seq,
    hidden,
    norm_gain,
    query_weight,
    key_weight,
    value_weight,
    output_weight,
    block_reach,
    header_ids,
):
    rows, width = hidden.shape
    head = key_weight.shape[1]
    n_line = n_seq // 2
    n_blocks = n_section * n_seq
    vmem = pl.BlockSpec(memory_space=pltpu.VMEM)
    smem = pl.BlockSpec(memory_space=pltpu.SMEM)
    anywhere = pl.BlockSpec(memory_space=pltpu.HBM)
    dma = pltpu.SemaphoreType.DMA
    bf16 = jnp.bfloat16
    f32 = jnp.float32
    attended = pl.pallas_call(
        functools.partial(fused, n_section, n_line),
        out_shape=jax.ShapeDtypeStruct((n_section, BLOCK, n_section * head), bf16),
        in_specs=[anywhere, vmem, anywhere, anywhere, anywhere, smem, smem],
        out_specs=vmem,
        scratch_shapes=[
            pltpu.VMEM((rows, width), bf16),
            pltpu.VMEM((rows, width), bf16),
            pltpu.VMEM((n_section, width, head), bf16),
            pltpu.VMEM((width, 2 * head), bf16),
            pltpu.VMEM((n_section, 8, BLOCK), f32),
            pltpu.VMEM((n_section, 8, BLOCK), f32),
            pltpu.VMEM((n_section, BLOCK, 2 * head), bf16),
            pltpu.VMEM((n_section, BLOCK, 2 * head), bf16),
            pltpu.VMEM((n_section, n_section, BLOCK, head), bf16),
            pltpu.VMEM((n_section, n_section, BLOCK, head), bf16),
            pltpu.VMEM((n_blocks, head, BLOCK), bf16),
            pltpu.VMEM((n_blocks, BLOCK, head), bf16),
            pltpu.VMEM((n_section * BLOCK, head), bf16),
            pltpu.VMEM((n_section * BLOCK, head), f32),
            pltpu.VMEM((n_section * BLOCK, head), f32),
            pltpu.VMEM((n_section * BLOCK, 2 * head), f32),
            pltpu.VMEM((n_section * BLOCK, 2 * n_section * BLOCK), f32),
            pltpu.VMEM((n_section * BLOCK, 2 * n_section * BLOCK), bf16),
            dma((5,)),
            dma((n_section,)),
            dma((n_section - 1,)),
            dma((n_section,)),
            dma((n_section - 1,)),
            dma((n_section,)),
            dma((n_section - 1,)),
            dma((n_section,)),
            dma((n_section - 1,)),
            dma((n_section,)),
            dma((n_section - 1,)),
            dma((n_section,)),
            dma((n_section, n_section - 1)),
            dma((n_section, n_section)),
            dma((n_line - 1,)),
            dma((n_line, n_section - 1)),
            dma((n_line, n_section)),
            dma((n_blocks,)),
            dma((n_section - 1,)),
            dma((n_section, n_line - 1)),
            dma((n_line, n_section)),
            dma((n_blocks,)),
            dma((n_section, n_section - 1)),
            dma((n_section, n_section)),
        ],
        compiler_params=pltpu.CompilerParams(
            collective_id=0, has_side_effects=True, vmem_limit_bytes=60 * 1024 * 1024
        ),
    )(
        hidden,
        norm_gain,
        query_weight,
        key_weight,
        value_weight,
        block_reach,
        header_ids,
    )
    return jnp.dot(
        attended.reshape(rows, n_section * head), output_weight, preferred_element_type=f32
    ).astype(bf16)


def solution(mesh):
    n_section, n_seq = mesh.shape["section"], mesh.shape["seq"]
    if n_section * n_seq <= FUSED_BLOCKS:
        program = functools.partial(on_device_fused, n_section, n_seq)
    else:
        program = on_device
    return jax.shard_map(
        program,
        mesh=mesh,
        in_specs=(
            P("seq", "section"),
            P("section"),
            P(None, "section"),
            P("section", None),
            P("section", None),
            P(None, "section"),
            P("seq"),
            P(),
        ),
        out_specs=P("seq", "section"),
        check_vma=False,
    )
```

```python
import functools
import math

import jax
import jax.numpy as jnp
from jax import lax
from jax.experimental import pallas as pl
from jax.experimental.pallas import tpu as pltpu
from jax.sharding import PartitionSpec as P

BLOCK = 128
REACH = 2


EPSILON = 1e-05
THETA = 500000.0


def merged(value, axis, combine):
    everything = jax.tree.map(lambda part: lax.all_gather(part, axis), value)
    leading = jax.tree.map(lambda part: part[0], everything)

    def lap(k, so_far):
        return combine(so_far, jax.tree.map(lambda part: part[k], everything))

    return lax.fori_loop(1, lax.axis_size(axis), lap, leading)


def padded(cells, sides, width):
    for axis, dim in sides:
        count = lax.axis_size(axis)
        ends = count - 1
        head = lax.slice_in_dim(cells, 0, width, axis=dim)
        tail = lax.slice_in_dim(cells, cells.shape[dim] - width, cells.shape[dim], axis=dim)
        cells = jnp.concatenate(
            [
                lax.ppermute(tail, axis, [(i, (i + 1) % count) for i in range(ends)]),
                cells,
                lax.ppermute(head, axis, [((i + 1) % count, i) for i in range(ends)]),
            ],
            axis=dim,
        )
    return cells


def tables(positions, head_width):
    middle = head_width // 2
    frequency = jnp.exp(
        -(2.0 / head_width) * math.log(THETA) * jnp.arange(middle, dtype=jnp.float32)
    )
    angles = positions.astype(jnp.float32)[:, None] * frequency[None, :]
    angles = jnp.concatenate([angles, angles], axis=1)
    return (jnp.cos(angles), jnp.sin(angles))


def rotate(values, cosine_table, sine_table):
    middle = values.shape[-1] // 2
    turned = jnp.concatenate([-values[..., middle:], values[..., :middle]], axis=-1)
    return values * cosine_table + turned * sine_table


def combine_parts(earlier, later):
    first_max, first_total, first_out = earlier
    second_max, second_total, second_out = later
    overall = jnp.maximum(first_max, second_max)
    first_factor = jnp.exp(first_max - overall)
    second_factor = jnp.exp(second_max - overall)
    return (
        overall,
        first_total * first_factor + second_total * second_factor,
        first_out * first_factor[:, None] + second_out * second_factor[:, None],
    )


def on_device(
    hidden,
    norm_gain,
    query_weight,
    key_weight,
    value_weight,
    output_weight,
    block_reach,
    header_ids,
):
    row_count = hidden.shape[0]
    part_width = hidden.shape[1]
    head_width = key_weight.shape[1]
    local_blocks = row_count // BLOCK
    total_blocks = local_blocks * lax.axis_size("seq")
    seq_place = lax.axis_index("seq")
    floats = hidden.astype(jnp.float32)
    squares = lax.psum(jnp.sum(floats * floats, axis=1), "section")
    scaling = lax.rsqrt(squares / (part_width * lax.axis_size("section")) + EPSILON)
    normed_part = (floats * scaling[:, None] * norm_gain.astype(jnp.float32)[None, :]).astype(
        jnp.bfloat16
    )
    weight_rows = query_weight
    query_sum = jnp.dot(
        lax.all_gather(normed_part, "section", axis=1, tiled=True),
        weight_rows,
        preferred_element_type=jnp.float32,
    )
    key_sum, value_sum = lax.psum(
        (
            jnp.dot(normed_part, key_weight, preferred_element_type=jnp.float32),
            jnp.dot(normed_part, value_weight, preferred_element_type=jnp.float32),
        ),
        "section",
    )
    positions = seq_place * row_count + jnp.arange(row_count, dtype=jnp.int32)
    cosine_table, sine_table = tables(positions, head_width)
    queries = rotate(query_sum, cosine_table, sine_table).astype(jnp.bfloat16)
    keys_here = rotate(key_sum, cosine_table, sine_table).astype(jnp.bfloat16)
    values_here = value_sum.astype(jnp.bfloat16)
    packed = jnp.concatenate([queries, keys_here, values_here], axis=1)
    block_numbers = seq_place * local_blocks + jnp.arange(local_blocks, dtype=jnp.int32)
    select = header_ids[:, None] == block_numbers[None, :]
    shaped = packed.reshape(local_blocks, BLOCK, 3 * head_width)
    picked = jnp.einsum(
        "hb,bre->hre", select.astype(jnp.bfloat16), shaped, preferred_element_type=jnp.float32
    )
    header_pack = lax.psum(picked, "seq").astype(jnp.bfloat16).reshape(-1, 3 * head_width)
    head_queries = header_pack[:, :head_width]
    head_keys = header_pack[:, head_width : 2 * head_width]
    head_values = header_pack[:, 2 * head_width :]
    inverse_root = 1.0 / math.sqrt(head_width)
    far_scores = (
        jnp.einsum("qd,kd->qk", head_queries, keys_here, preferred_element_type=jnp.float32)
        * inverse_root
    )
    far_max = jnp.max(far_scores, axis=1)
    far_weights = jnp.exp(far_scores - far_max[:, None])
    far_total = jnp.sum(far_weights, axis=1)
    far_out = jnp.dot(
        far_weights.astype(jnp.bfloat16), values_here, preferred_element_type=jnp.float32
    )
    merged_max, merged_total, merged_out = merged(
        (far_max, far_total, far_out), "seq", combine_parts
    )
    header_result = merged_out / merged_total[:, None]
    margin_rows = REACH * BLOCK
    stacked = jnp.concatenate([keys_here, values_here], axis=1)
    extended = padded(stacked, (("seq", 0),), margin_rows)
    near_keys = extended[:, :head_width]
    near_values = extended[:, head_width:]
    extent = row_count + 2 * margin_rows
    key_blocks = seq_place * local_blocks - REACH + jnp.arange(extent, dtype=jnp.int32) // BLOCK
    query_blocks = seq_place * local_blocks + jnp.arange(row_count, dtype=jnp.int32) // BLOCK
    limits = jnp.repeat(block_reach, BLOCK)
    key_header = jnp.any(header_ids[:, None] == key_blocks[None, :], axis=0)
    allowed = (key_blocks >= 0)[None, :] & (key_blocks < total_blocks)[None, :]
    allowed = allowed & (jnp.abs(key_blocks[None, :] - query_blocks[:, None]) <= limits[:, None])
    allowed = allowed & jnp.logical_not(key_header)[None, :]
    near_scores = (
        jnp.einsum("qd,kd->qk", queries, near_keys, preferred_element_type=jnp.float32)
        * inverse_root
    )
    near_scores = jnp.where(allowed, near_scores, -jnp.inf)
    head_scores = (
        jnp.einsum("qd,kd->qk", queries, head_keys, preferred_element_type=jnp.float32)
        * inverse_root
    )
    scores = jnp.concatenate([near_scores, head_scores], axis=1)
    row_top = jnp.max(scores, axis=1)
    weights = jnp.exp(scores - row_top[:, None])
    row_sums = jnp.sum(weights, axis=1)
    joined = jnp.concatenate([near_values, head_values], axis=0)
    mixed_out = (
        jnp.dot(weights.astype(jnp.bfloat16), joined, preferred_element_type=jnp.float32)
        / row_sums[:, None]
    )
    header_local = jnp.einsum(
        "hb,hre->bre", select.astype(jnp.float32), header_result.reshape(-1, BLOCK, head_width)
    )
    is_local_header = jnp.any(select, axis=0)
    attended = jnp.where(
        is_local_header[:, None, None],
        header_local,
        mixed_out.reshape(local_blocks, BLOCK, head_width),
    )
    attended = attended.reshape(row_count, head_width).astype(jnp.bfloat16)
    weight_rows = output_weight
    result = jnp.dot(
        lax.all_gather(attended, "section", axis=1, tiled=True),
        weight_rows,
        preferred_element_type=jnp.float32,
    )
    return result.astype(jnp.bfloat16)


MESH = pl.DeviceIdType.MESH
LOW = -1e30
FUSED_BLOCKS = 64


def fused(
    n_section,
    n_line,
    hidden_ref,
    gain_ref,
    query_ref,
    key_ref,
    value_ref,
    project_ref,
    reach_ref,
    ids_ref,
    out_ref,
    x,
    scaled,
    wq,
    wkv,
    squares,
    squares_got,
    kv_part,
    kv_got,
    q_part,
    q_got,
    key_blocks,
    value_blocks,
    queries,
    top,
    fade,
    acc,
    scores,
    weights,
    attended,
    wo,
    result,
    local_sem,
    x_sem,
    w_send,
    w_recv,
    wz_send,
    wz_recv,
    wf_send,
    wf_recv,
    sq_send,
    sq_recv,
    kv_send,
    kv_recv,
    q_send,
    q_recv,
    line_send,
    plane_send,
    twin_send,
    key_recv,
    key_twin_recv,
    value_plane_send,
    value_line_send,
    value_twin_send,
    value_recv,
    value_line_recv,
    value_twin_recv,
    out_send,
    out_recv,
    store_sem,
):
    width = x.shape[1]
    half = width // 2
    head = wq.shape[2]
    s = lax.axis_index("section")
    j = lax.axis_index("seq")
    z = j // 2
    c = j % 2
    twin = z * 2 + (1 - c)
    others = [(s + k) % n_section for k in range(1, n_section)]
    line = [((z + k) % n_line) * 2 + c for k in range(1, n_line)]

    def push(src, dst, send, recv, section, seq):
        copy = pltpu.make_async_remote_copy(
            src_ref=src,
            dst_ref=dst,
            send_sem=send,
            recv_sem=recv,
            device_id=(section, seq),
            device_id_type=MESH,
        )
        copy.start()
        pending.append(copy)

    def arrived(dst, recv):
        pltpu.make_async_remote_copy(
            src_ref=dst,
            dst_ref=dst,
            send_sem=local_sem.at[4],
            recv_sem=recv,
            device_id=(s, twin),
            device_id_type=MESH,
        ).wait_recv()

    pending = []
    get_x = []
    for r in range(n_section):
        rows = pl.ds(r * BLOCK, BLOCK)
        get_x.append(pltpu.make_async_copy(hidden_ref.at[rows, :], x.at[rows, :], x_sem.at[r]))
        get_x[r].start()
    get_k = pltpu.make_async_copy(key_ref, wkv.at[:, 0:head], local_sem.at[1])
    get_v = pltpu.make_async_copy(value_ref, wkv.at[:, head : 2 * head], local_sem.at[2])
    get_q = pltpu.make_async_copy(
        query_ref.at[pl.ds(pl.multiple_of(s * width, width), width), :], wq.at[s], local_sem.at[3]
    )
    get_o = pltpu.make_async_copy(project_ref, wo, local_sem.at[0])
    get_k.start()
    get_v.start()
    get_q.start()
    get_o.start()

    barrier = pltpu.get_barrier_semaphore()
    friends = [(t, j) for t in others] + [(s, i) for i in line] + [(s, twin)]
    for friend in friends:
        pl.semaphore_signal(barrier, inc=1, device_id=friend, device_id_type=MESH)

    pl.semaphore_wait(barrier, len(friends))

    quarter = half // 2
    partner = (z + 1 - 2 * (z % 2)) * 2 + c
    mine = pl.ds(pl.multiple_of(c * half, half), half)
    near = pl.ds(pl.multiple_of(c * half + (z % 2) * quarter, quarter), quarter)
    far = pl.ds(pl.multiple_of(c * half + (1 - z % 2) * quarter, quarter), quarter)
    for k, t in enumerate(others):
        push(
            query_ref.at[
                pl.ds(
                    pl.multiple_of(t * width + c * half + (z % 2) * quarter, quarter), quarter
                ),
                :,
            ],
            wq.at[s, near, :],
            w_send.at[k],
            w_recv.at[s],
            t,
            j,
        )

    gain = gain_ref[...].astype(jnp.float32).reshape(1, width)
    for r in range(n_section):
        get_x[r].wait()
        part = x[r * BLOCK : (r + 1) * BLOCK, :].astype(jnp.float32)
        scaled[r * BLOCK : (r + 1) * BLOCK, :] = (part * gain).astype(jnp.bfloat16)
    get_k.wait()
    get_v.wait()
    kv_part[...] = (
        jnp.dot(scaled[...], wkv[...], preferred_element_type=jnp.float32)
        .astype(jnp.bfloat16)
        .reshape(kv_part.shape)
    )
    for k, t in enumerate(others):
        push(kv_part.at[t], kv_got.at[s], kv_send.at[k], kv_recv.at[s], t, j)

    for r in range(n_section):
        part = x[r * BLOCK : (r + 1) * BLOCK, :].astype(jnp.float32)
        column = jnp.sum(part * part, axis=1, keepdims=True)
        squares[r] = jnp.transpose(jnp.broadcast_to(column, (BLOCK, BLOCK)))[:8, :]
    for k, t in enumerate(others):
        push(squares.at[t], squares_got.at[s], sq_send.at[k], sq_recv.at[s], t, j)

    b = j * n_section + s
    lanes = lax.broadcasted_iota(jnp.int32, (BLOCK, head), 1)
    positions = b * BLOCK + lax.broadcasted_iota(jnp.int32, (BLOCK, head), 0)
    spots = lax.rem(lanes, head // 2).astype(jnp.float32)
    angles = positions.astype(jnp.float32) * jnp.exp(-(2.0 / head) * math.log(THETA) * spots)
    cosine = jnp.cos(angles)
    sine = jnp.where(lanes < head // 2, -1.0, 1.0) * jnp.sin(angles)

    def project(k):
        owner = (s + k) % n_section
        q_part[:, k] = (
            jnp.dot(scaled[...], wq[owner], preferred_element_type=jnp.float32)
            .astype(jnp.bfloat16)
            .reshape(n_section, BLOCK, head)
        )

    get_q.wait()
    project(0)
    for k, t in enumerate(others):
        push(q_part.at[t, 0], q_got.at[s, 0], q_send.at[0, k], q_recv.at[s, 0], t, j)
    for k, t in enumerate(others):
        arrived(wq.at[t, near, :], w_recv.at[t])
        push(wq.at[t, near, :], wq.at[t, near, :], wz_send.at[k], wz_recv.at[t], s, partner)

    def turned(values):
        return values * cosine + pltpu.roll(values, head // 2, axis=1) * sine

    for t in others:
        arrived(squares_got.at[t], sq_recv.at[t])
    sums = squares[s]
    for t in others:
        sums = sums + squares_got[t]
    scaling = lax.rsqrt(sums / (width * n_section) + EPSILON)
    scaling = jnp.transpose(jnp.broadcast_to(scaling[0:1, :], (BLOCK, BLOCK)))
    for t in others:
        arrived(kv_got.at[t], kv_recv.at[t])
    kv = kv_part[s].astype(jnp.float32)
    for t in others:
        kv = kv + kv_got[t].astype(jnp.float32)
    key_blocks[b] = jnp.transpose(turned(kv[:, :head] * scaling)).astype(jnp.bfloat16)
    value_blocks[b] = (kv[:, head:] * scaling).astype(jnp.bfloat16)

    across = s + 1 - 2 * (s % 2)
    along = (s + 2) % n_section
    corner = (across + 2) % n_section
    relayed = jnp.where(c == 0, across, along)
    direct = jnp.where(c == 0, along, across)

    def hand_key(number, send, section, seq):
        piece = key_blocks.at[number]
        push(piece, piece, send, key_recv.at[number], section, seq)

    def hand_value(number, send, section):
        piece = value_blocks.at[number]
        push(piece, piece, send, value_recv.at[number - j * n_section], section, j)

    def await_key(number):
        arrived(key_blocks.at[number], key_recv.at[number])

    def await_value(number):
        arrived(value_blocks.at[number], value_recv.at[number - j * n_section])

    def plane(blocks, seq):
        return blocks.at[pl.ds(seq * n_section, n_section)]

    def spread_key(number, slot):
        hand_key(number, plane_send.at[slot, 0], relayed, j)
        hand_key(number, plane_send.at[slot, 1], direct, j)

    def relay_key(slot, seq):
        number = seq * n_section + relayed
        await_key(number)
        hand_key(number, plane_send.at[slot, 2], direct, j)

    for k, i in enumerate(line):
        hand_key(b, line_send.at[k], s, i)
    hand_value(b, value_plane_send.at[0], relayed)
    hand_value(b, value_plane_send.at[1], direct)
    spread_key(b, 0)

    number = j * n_section + relayed
    await_value(number)
    hand_value(number, value_plane_send.at[2], direct)
    for k, t in enumerate(others):
        arrived(wq.at[t, far, :], wz_recv.at[t])
        push(wq.at[t, mine, :], wq.at[t, mine, :], wf_send.at[k], wf_recv.at[t], s, twin)
    for k, i in enumerate(line):
        number = i * n_section + s
        await_key(number)
        spread_key(number, k + 1)
    await_value(j * n_section + direct)
    await_value(j * n_section + corner)
    whole = plane(value_blocks, j)
    for k, i in enumerate(line):
        push(whole, whole, value_line_send.at[k], value_line_recv.at[z], s, i)
    push(whole, whole, value_twin_send.at[0], value_twin_recv.at[z], s, twin)
    theirs = pl.ds(pl.multiple_of((1 - c) * half, half), half)
    for k, t in enumerate(others):
        arrived(wq.at[t, theirs, :], wf_recv.at[t])
        project(k + 1)
    rest = pl.ds(1, n_section - 1)
    for k, t in enumerate(others):
        push(q_part.at[t, rest], q_got.at[s, rest], q_send.at[1, k], q_recv.at[s, 1], t, j)
    relay_key(0, j)
    for k, i in enumerate(line):
        relay_key(k + 1, i)

    for t in others:
        arrived(q_got.at[t, 0], q_recv.at[t, 0])
        arrived(q_got.at[t, rest], q_recv.at[t, 1])
    for h in range(n_section):
        place = (h + n_section - s) % n_section
        value = q_part[s, place].astype(jnp.float32)
        for t in others:
            value = value + q_got[t, (h + n_section - t) % n_section].astype(jnp.float32)
        queries[h * BLOCK : (h + 1) * BLOCK, :] = turned(value * scaling).astype(jnp.bfloat16)

    first = ids_ref[0]
    second = ids_ref[1]
    own_header = jnp.logical_or(first == b, second == b)
    limit = jnp.where(own_header, n_section * n_line * 2, reach_ref[s])
    group = 2 * n_section
    keys_wide = group * BLOCK
    factor = 1.4426950408889634 / math.sqrt(head)
    top[...] = jnp.full(top.shape, LOW, jnp.float32)
    acc[...] = jnp.zeros(acc.shape, jnp.float32)
    ones = jnp.ones((keys_wide, head), jnp.bfloat16)
    strip = 32

    def attend(place):
        start = place * group
        numbers = start + lax.broadcasted_iota(jnp.int32, (1, keys_wide), 1) // BLOCK
        valid = (numbers == first) | (numbers == second) | (jnp.abs(numbers - b) <= limit)
        bias = jnp.where(valid, 0.0, LOW)
        keys = jnp.concatenate([key_blocks[start + n] for n in range(group)], axis=1)
        scores[...] = jnp.dot(queries[...], keys, preferred_element_type=jnp.float32)
        for r in range(0, n_section * BLOCK, strip):
            rows = pl.ds(r, strip)
            part = scores[rows, :] * factor + bias
            before = top[rows, :]
            after = jnp.maximum(before, jnp.max(part, axis=1, keepdims=True))
            weights[rows, :] = jnp.exp2(part - after[:, 0:1]).astype(jnp.bfloat16)
            fade[rows, :] = jnp.exp2(before - after)
            top[rows, :] = after
        values = value_blocks[pl.ds(start, group)].reshape(keys_wide, head)
        gained = jnp.dot(
            weights[...],
            jnp.concatenate([values, ones], axis=1),
            preferred_element_type=jnp.float32,
        )
        factors = fade[...]
        acc[:, 0:head] = acc[:, 0:head] * factors + gained[:, 0:head]
        acc[:, head : 2 * head] = acc[:, head : 2 * head] * factors + gained[:, head : 2 * head]

    def pass_on(i):
        place = (z + i) % n_line
        seq = place * 2 + c
        for t in (direct, corner):
            await_key(seq * n_section + t)
        keys = plane(key_blocks, seq)
        push(keys, keys, twin_send.at[i], key_twin_recv.at[place], s, twin)
        if i > 0:
            values = plane(value_blocks, seq)
            arrived(values, value_line_recv.at[place])
            push(values, values, value_twin_send.at[i], value_twin_recv.at[place], s, twin)

    pass_on(0)
    for i in range(n_line):
        if i + 1 < n_line:
            pass_on(i + 1)
        place = (z + i) % n_line
        seq = place * 2 + 1 - c
        arrived(plane(key_blocks, seq), key_twin_recv.at[place])
        arrived(plane(value_blocks, seq), value_twin_recv.at[place])
        attend(place)

    for h in range(n_section):
        rows = pl.ds(h * BLOCK, BLOCK)
        attended[s, :, h * head : (h + 1) * head] = (
            acc[rows, 0:head] / acc[rows, head : 2 * head]
        ).astype(jnp.bfloat16)
    for k, t in enumerate(others):
        push(attended.at[s], attended.at[s], out_send.at[k], out_recv.at[s], t, j)
    get_o.wait()

    def finish(owner, k):
        rows = pl.ds(pl.multiple_of(owner * BLOCK, BLOCK), BLOCK)
        result[rows, :] = jnp.dot(
            attended[owner], wo[...], preferred_element_type=jnp.float32
        ).astype(jnp.bfloat16)
        copy = pltpu.make_async_copy(result.at[rows, :], out_ref.at[rows, :], store_sem.at[k])
        copy.start()
        return copy

    stores = [finish(s, 0)]
    for k, t in enumerate([across, along, corner]):
        arrived(attended.at[t], out_recv.at[t])
        stores.append(finish(t, k + 1))
    for copy in stores:
        copy.wait()
    for copy in pending:
        copy.wait_send()


def on_device_fused(
    n_section,
    n_seq,
    hidden,
    norm_gain,
    query_weight,
    key_weight,
    value_weight,
    output_weight,
    block_reach,
    header_ids,
):
    rows, width = hidden.shape
    head = key_weight.shape[1]
    n_line = n_seq // 2
    n_blocks = n_section * n_seq
    vmem = pl.BlockSpec(memory_space=pltpu.VMEM)
    smem = pl.BlockSpec(memory_space=pltpu.SMEM)
    anywhere = pl.BlockSpec(memory_space=pltpu.HBM)
    dma = pltpu.SemaphoreType.DMA
    bf16 = jnp.bfloat16
    f32 = jnp.float32
    return pl.pallas_call(
        functools.partial(fused, n_section, n_line),
        out_shape=jax.ShapeDtypeStruct((rows, width), bf16),
        in_specs=[anywhere, vmem, anywhere, anywhere, anywhere, anywhere, smem, smem],
        out_specs=anywhere,
        scratch_shapes=[
            pltpu.VMEM((rows, width), bf16),
            pltpu.VMEM((rows, width), bf16),
            pltpu.VMEM((n_section, width, head), bf16),
            pltpu.VMEM((width, 2 * head), bf16),
            pltpu.VMEM((n_section, 8, BLOCK), f32),
            pltpu.VMEM((n_section, 8, BLOCK), f32),
            pltpu.VMEM((n_section, BLOCK, 2 * head), bf16),
            pltpu.VMEM((n_section, BLOCK, 2 * head), bf16),
            pltpu.VMEM((n_section, n_section, BLOCK, head), bf16),
            pltpu.VMEM((n_section, n_section, BLOCK, head), bf16),
            pltpu.VMEM((n_blocks, head, BLOCK), bf16),
            pltpu.VMEM((n_blocks, BLOCK, head), bf16),
            pltpu.VMEM((n_section * BLOCK, head), bf16),
            pltpu.VMEM((n_section * BLOCK, head), f32),
            pltpu.VMEM((n_section * BLOCK, head), f32),
            pltpu.VMEM((n_section * BLOCK, 2 * head), f32),
            pltpu.VMEM((n_section * BLOCK, 2 * n_section * BLOCK), f32),
            pltpu.VMEM((n_section * BLOCK, 2 * n_section * BLOCK), bf16),
            pltpu.VMEM((n_section, BLOCK, n_section * head), bf16),
            pltpu.VMEM((n_section * head, width), bf16),
            pltpu.VMEM((rows, width), bf16),
            dma((5,)),
            dma((n_section,)),
            dma((n_section - 1,)),
            dma((n_section,)),
            dma((n_section - 1,)),
            dma((n_section,)),
            dma((n_section - 1,)),
            dma((n_section,)),
            dma((n_section - 1,)),
            dma((n_section,)),
            dma((n_section - 1,)),
            dma((n_section,)),
            dma((2, n_section - 1)),
            dma((n_section, 2)),
            dma((n_line - 1,)),
            dma((n_line, n_section - 1)),
            dma((n_line,)),
            dma((n_blocks,)),
            dma((n_line,)),
            dma((n_section - 1,)),
            dma((n_line - 1,)),
            dma((n_line,)),
            dma((n_section,)),
            dma((n_line,)),
            dma((n_line,)),
            dma((n_section - 1,)),
            dma((n_section,)),
            dma((n_section,)),
        ],
        compiler_params=pltpu.CompilerParams(
            collective_id=0, has_side_effects=True, vmem_limit_bytes=60 * 1024 * 1024
        ),
    )(
        hidden,
        norm_gain,
        query_weight,
        key_weight,
        value_weight,
        output_weight,
        block_reach,
        header_ids,
    )

def solution(mesh):
    n_section, n_seq = mesh.shape["section"], mesh.shape["seq"]
    if n_section * n_seq <= FUSED_BLOCKS:
        program = functools.partial(on_device_fused, n_section, n_seq)
    else:
        program = on_device
    return jax.shard_map(
        program,
        mesh=mesh,
        in_specs=(
            P("seq", "section"),
            P("section"),
            P(None, "section"),
            P("section", None),
            P("section", None),
            P(None, "section"),
            P("seq"),
            P(),
        ),
        out_specs=P("seq", "section"),
        check_vma=False,
    )
```

```python
import functools
import math

import jax
import jax.numpy as jnp
from jax import lax
from jax.experimental import pallas as pl
from jax.experimental.pallas import tpu as pltpu
from jax.sharding import PartitionSpec as P

BLOCK = 128
REACH = 2


EPSILON = 1e-05
THETA = 500000.0


def merged(value, axis, combine):
    everything = jax.tree.map(lambda part: lax.all_gather(part, axis), value)
    leading = jax.tree.map(lambda part: part[0], everything)

    def lap(k, so_far):
        return combine(so_far, jax.tree.map(lambda part: part[k], everything))

    return lax.fori_loop(1, lax.axis_size(axis), lap, leading)


def padded(cells, sides, width):
    for axis, dim in sides:
        count = lax.axis_size(axis)
        ends = count - 1
        head = lax.slice_in_dim(cells, 0, width, axis=dim)
        tail = lax.slice_in_dim(cells, cells.shape[dim] - width, cells.shape[dim], axis=dim)
        cells = jnp.concatenate(
            [
                lax.ppermute(tail, axis, [(i, (i + 1) % count) for i in range(ends)]),
                cells,
                lax.ppermute(head, axis, [((i + 1) % count, i) for i in range(ends)]),
            ],
            axis=dim,
        )
    return cells


def tables(positions, head_width):
    middle = head_width // 2
    frequency = jnp.exp(
        -(2.0 / head_width) * math.log(THETA) * jnp.arange(middle, dtype=jnp.float32)
    )
    angles = positions.astype(jnp.float32)[:, None] * frequency[None, :]
    angles = jnp.concatenate([angles, angles], axis=1)
    return (jnp.cos(angles), jnp.sin(angles))


def rotate(values, cosine_table, sine_table):
    middle = values.shape[-1] // 2
    turned = jnp.concatenate([-values[..., middle:], values[..., :middle]], axis=-1)
    return values * cosine_table + turned * sine_table


def combine_parts(earlier, later):
    first_max, first_total, first_out = earlier
    second_max, second_total, second_out = later
    overall = jnp.maximum(first_max, second_max)
    first_factor = jnp.exp(first_max - overall)
    second_factor = jnp.exp(second_max - overall)
    return (
        overall,
        first_total * first_factor + second_total * second_factor,
        first_out * first_factor[:, None] + second_out * second_factor[:, None],
    )


def on_device(
    hidden,
    norm_gain,
    query_weight,
    key_weight,
    value_weight,
    output_weight,
    block_reach,
    header_ids,
):
    row_count = hidden.shape[0]
    part_width = hidden.shape[1]
    head_width = key_weight.shape[1]
    local_blocks = row_count // BLOCK
    total_blocks = local_blocks * lax.axis_size("seq")
    seq_place = lax.axis_index("seq")
    floats = hidden.astype(jnp.float32)
    squares = lax.psum(jnp.sum(floats * floats, axis=1), "section")
    scaling = lax.rsqrt(squares / (part_width * lax.axis_size("section")) + EPSILON)
    normed_part = (floats * scaling[:, None] * norm_gain.astype(jnp.float32)[None, :]).astype(
        jnp.bfloat16
    )
    weight_rows = query_weight
    query_sum = jnp.dot(
        lax.all_gather(normed_part, "section", axis=1, tiled=True),
        weight_rows,
        preferred_element_type=jnp.float32,
    )
    key_sum, value_sum = lax.psum(
        (
            jnp.dot(normed_part, key_weight, preferred_element_type=jnp.float32),
            jnp.dot(normed_part, value_weight, preferred_element_type=jnp.float32),
        ),
        "section",
    )
    positions = seq_place * row_count + jnp.arange(row_count, dtype=jnp.int32)
    cosine_table, sine_table = tables(positions, head_width)
    queries = rotate(query_sum, cosine_table, sine_table).astype(jnp.bfloat16)
    keys_here = rotate(key_sum, cosine_table, sine_table).astype(jnp.bfloat16)
    values_here = value_sum.astype(jnp.bfloat16)
    packed = jnp.concatenate([queries, keys_here, values_here], axis=1)
    block_numbers = seq_place * local_blocks + jnp.arange(local_blocks, dtype=jnp.int32)
    select = header_ids[:, None] == block_numbers[None, :]
    shaped = packed.reshape(local_blocks, BLOCK, 3 * head_width)
    picked = jnp.einsum(
        "hb,bre->hre", select.astype(jnp.bfloat16), shaped, preferred_element_type=jnp.float32
    )
    header_pack = lax.psum(picked, "seq").astype(jnp.bfloat16).reshape(-1, 3 * head_width)
    head_queries = header_pack[:, :head_width]
    head_keys = header_pack[:, head_width : 2 * head_width]
    head_values = header_pack[:, 2 * head_width :]
    inverse_root = 1.0 / math.sqrt(head_width)
    far_scores = (
        jnp.einsum("qd,kd->qk", head_queries, keys_here, preferred_element_type=jnp.float32)
        * inverse_root
    )
    far_max = jnp.max(far_scores, axis=1)
    far_weights = jnp.exp(far_scores - far_max[:, None])
    far_total = jnp.sum(far_weights, axis=1)
    far_out = jnp.dot(
        far_weights.astype(jnp.bfloat16), values_here, preferred_element_type=jnp.float32
    )
    merged_max, merged_total, merged_out = merged(
        (far_max, far_total, far_out), "seq", combine_parts
    )
    header_result = merged_out / merged_total[:, None]
    margin_rows = REACH * BLOCK
    stacked = jnp.concatenate([keys_here, values_here], axis=1)
    extended = padded(stacked, (("seq", 0),), margin_rows)
    near_keys = extended[:, :head_width]
    near_values = extended[:, head_width:]
    extent = row_count + 2 * margin_rows
    key_blocks = seq_place * local_blocks - REACH + jnp.arange(extent, dtype=jnp.int32) // BLOCK
    query_blocks = seq_place * local_blocks + jnp.arange(row_count, dtype=jnp.int32) // BLOCK
    limits = jnp.repeat(block_reach, BLOCK)
    key_header = jnp.any(header_ids[:, None] == key_blocks[None, :], axis=0)
    allowed = (key_blocks >= 0)[None, :] & (key_blocks < total_blocks)[None, :]
    allowed = allowed & (jnp.abs(key_blocks[None, :] - query_blocks[:, None]) <= limits[:, None])
    allowed = allowed & jnp.logical_not(key_header)[None, :]
    near_scores = (
        jnp.einsum("qd,kd->qk", queries, near_keys, preferred_element_type=jnp.float32)
        * inverse_root
    )
    near_scores = jnp.where(allowed, near_scores, -jnp.inf)
    head_scores = (
        jnp.einsum("qd,kd->qk", queries, head_keys, preferred_element_type=jnp.float32)
        * inverse_root
    )
    scores = jnp.concatenate([near_scores, head_scores], axis=1)
    row_top = jnp.max(scores, axis=1)
    weights = jnp.exp(scores - row_top[:, None])
    row_sums = jnp.sum(weights, axis=1)
    joined = jnp.concatenate([near_values, head_values], axis=0)
    mixed_out = (
        jnp.dot(weights.astype(jnp.bfloat16), joined, preferred_element_type=jnp.float32)
        / row_sums[:, None]
    )
    header_local = jnp.einsum(
        "hb,hre->bre", select.astype(jnp.float32), header_result.reshape(-1, BLOCK, head_width)
    )
    is_local_header = jnp.any(select, axis=0)
    attended = jnp.where(
        is_local_header[:, None, None],
        header_local,
        mixed_out.reshape(local_blocks, BLOCK, head_width),
    )
    attended = attended.reshape(row_count, head_width).astype(jnp.bfloat16)
    weight_rows = output_weight
    result = jnp.dot(
        lax.all_gather(attended, "section", axis=1, tiled=True),
        weight_rows,
        preferred_element_type=jnp.float32,
    )
    return result.astype(jnp.bfloat16)


MESH = pl.DeviceIdType.MESH
LOW = -1e30
FUSED_BLOCKS = 64


def fused(
    n_section,
    n_line,
    hidden_ref,
    gain_ref,
    query_ref,
    key_ref,
    value_ref,
    project_ref,
    reach_ref,
    ids_ref,
    out_ref,
    x,
    scaled,
    wq,
    wkv,
    squares,
    squares_got,
    kv_part,
    kv_got,
    q_part,
    q_got,
    key_blocks,
    value_blocks,
    queries,
    top,
    fade,
    acc,
    scores,
    weights,
    attended,
    wo,
    result,
    local_sem,
    x_sem,
    w_send,
    w_recv,
    wz_send,
    wz_recv,
    wf_send,
    wf_recv,
    sq_send,
    sq_recv,
    kv_send,
    kv_recv,
    q_send,
    q_recv,
    line_send,
    plane_send,
    twin_send,
    key_recv,
    key_twin_recv,
    value_plane_send,
    value_line_send,
    value_twin_send,
    value_recv,
    value_line_recv,
    value_twin_recv,
    out_send,
    out_recv,
    store_sem,
):
    width = x.shape[1]
    half = width // 2
    head = wq.shape[2]
    s = lax.axis_index("section")
    j = lax.axis_index("seq")
    z = j // 2
    c = j % 2
    twin = z * 2 + (1 - c)
    others = [(s + k) % n_section for k in range(1, n_section)]
    line = [((z + k) % n_line) * 2 + c for k in range(1, n_line)]

    def push(src, dst, send, recv, section, seq):
        copy = pltpu.make_async_remote_copy(
            src_ref=src,
            dst_ref=dst,
            send_sem=send,
            recv_sem=recv,
            device_id=(section, seq),
            device_id_type=MESH,
        )
        copy.start()
        pending.append(copy)

    def arrived(dst, recv):
        pltpu.make_async_remote_copy(
            src_ref=dst,
            dst_ref=dst,
            send_sem=local_sem.at[4],
            recv_sem=recv,
            device_id=(s, twin),
            device_id_type=MESH,
        ).wait_recv()

    pending = []
    get_x = []
    for r in range(n_section):
        rows = pl.ds(r * BLOCK, BLOCK)
        get_x.append(pltpu.make_async_copy(hidden_ref.at[rows, :], x.at[rows, :], x_sem.at[r]))
        get_x[r].start()
    get_k = pltpu.make_async_copy(key_ref, wkv.at[:, 0:head], local_sem.at[1])
    get_v = pltpu.make_async_copy(value_ref, wkv.at[:, head : 2 * head], local_sem.at[2])
    get_q = pltpu.make_async_copy(
        query_ref.at[pl.ds(pl.multiple_of(s * width, width), width), :], wq.at[s], local_sem.at[3]
    )
    get_o = pltpu.make_async_copy(project_ref, wo, local_sem.at[0])
    get_k.start()
    get_v.start()
    get_q.start()
    get_o.start()

    barrier = pltpu.get_barrier_semaphore()
    friends = [(t, j) for t in others] + [(s, i) for i in line] + [(s, twin)]
    for friend in friends:
        pl.semaphore_signal(barrier, inc=1, device_id=friend, device_id_type=MESH)

    pl.semaphore_wait(barrier, len(friends))

    quarter = half // 2
    partner = (z + 1 - 2 * (z % 2)) * 2 + c
    mine = pl.ds(pl.multiple_of(c * half, half), half)
    near = pl.ds(pl.multiple_of(c * half + (z % 2) * quarter, quarter), quarter)
    far = pl.ds(pl.multiple_of(c * half + (1 - z % 2) * quarter, quarter), quarter)
    for k, t in enumerate(others):
        push(
            query_ref.at[
                pl.ds(
                    pl.multiple_of(t * width + c * half + (z % 2) * quarter, quarter), quarter
                ),
                :,
            ],
            wq.at[s, near, :],
            w_send.at[k],
            w_recv.at[s],
            t,
            j,
        )

    gain = gain_ref[...].astype(jnp.float32).reshape(1, width)
    for r in range(n_section):
        get_x[r].wait()
        part = x[r * BLOCK : (r + 1) * BLOCK, :].astype(jnp.float32)
        scaled[r * BLOCK : (r + 1) * BLOCK, :] = (part * gain).astype(jnp.bfloat16)
    get_k.wait()
    get_v.wait()
    kv_part[...] = (
        jnp.dot(scaled[...], wkv[...], preferred_element_type=jnp.float32)
        .astype(jnp.bfloat16)
        .reshape(kv_part.shape)
    )
    for k, t in enumerate(others):
        push(kv_part.at[t], kv_got.at[s], kv_send.at[k], kv_recv.at[s], t, j)

    for r in range(n_section):
        part = x[r * BLOCK : (r + 1) * BLOCK, :].astype(jnp.float32)
        column = jnp.sum(part * part, axis=1, keepdims=True)
        squares[r] = jnp.transpose(jnp.broadcast_to(column, (BLOCK, BLOCK)))[:8, :]
    for k, t in enumerate(others):
        push(squares.at[t], squares_got.at[s], sq_send.at[k], sq_recv.at[s], t, j)

    b = j * n_section + s
    lanes = lax.broadcasted_iota(jnp.int32, (BLOCK, head), 1)
    positions = b * BLOCK + lax.broadcasted_iota(jnp.int32, (BLOCK, head), 0)
    spots = lax.rem(lanes, head // 2).astype(jnp.float32)
    angles = positions.astype(jnp.float32) * jnp.exp(-(2.0 / head) * math.log(THETA) * spots)
    cosine = jnp.cos(angles)
    sine = jnp.where(lanes < head // 2, -1.0, 1.0) * jnp.sin(angles)

    def project(k):
        owner = (s + k) % n_section
        q_part[:, k] = (
            jnp.dot(scaled[...], wq[owner], preferred_element_type=jnp.float32)
            .astype(jnp.bfloat16)
            .reshape(n_section, BLOCK, head)
        )

    get_q.wait()
    project(0)
    for k, t in enumerate(others):
        push(q_part.at[t, 0], q_got.at[s, 0], q_send.at[0, k], q_recv.at[s, 0], t, j)
    for k, t in enumerate(others):
        arrived(wq.at[t, near, :], w_recv.at[t])
        push(wq.at[t, near, :], wq.at[t, near, :], wz_send.at[k], wz_recv.at[t], s, partner)

    def turned(values):
        return values * cosine + pltpu.roll(values, head // 2, axis=1) * sine

    for t in others:
        arrived(squares_got.at[t], sq_recv.at[t])
    sums = squares[s]
    for t in others:
        sums = sums + squares_got[t]
    scaling = lax.rsqrt(sums / (width * n_section) + EPSILON)
    scaling = jnp.transpose(jnp.broadcast_to(scaling[0:1, :], (BLOCK, BLOCK)))
    for t in others:
        arrived(kv_got.at[t], kv_recv.at[t])
    kv = kv_part[s].astype(jnp.float32)
    for t in others:
        kv = kv + kv_got[t].astype(jnp.float32)
    key_blocks[b] = jnp.transpose(turned(kv[:, :head] * scaling)).astype(jnp.bfloat16)
    value_blocks[b] = (kv[:, head:] * scaling).astype(jnp.bfloat16)

    across = s + 1 - 2 * (s % 2)
    along = (s + 2) % n_section
    corner = (across + 2) % n_section
    peers = [across, along, corner]

    def hand_key(number, send, section, seq):
        piece = key_blocks.at[number]
        push(piece, piece, send, key_recv.at[number], section, seq)

    def hand_value(number, send, section):
        piece = value_blocks.at[number]
        push(piece, piece, send, value_recv.at[number - j * n_section], section, j)

    def await_key(number):
        arrived(key_blocks.at[number], key_recv.at[number])

    def await_value(number):
        arrived(value_blocks.at[number], value_recv.at[number - j * n_section])

    def plane(blocks, seq):
        return blocks.at[pl.ds(seq * n_section, n_section)]

    def spread_key(number, slot):
        for k, t in enumerate(peers):
            hand_key(number, plane_send.at[slot, k], t, j)

    for k, i in enumerate(line):
        hand_key(b, line_send.at[k], s, i)
    for k, t in enumerate(peers):
        hand_value(b, value_plane_send.at[k], t)
    spread_key(b, 0)

    for k, t in enumerate(others):
        arrived(wq.at[t, far, :], wz_recv.at[t])
        push(wq.at[t, mine, :], wq.at[t, mine, :], wf_send.at[k], wf_recv.at[t], s, twin)
    for k, i in enumerate(line):
        number = i * n_section + s
        await_key(number)
        spread_key(number, k + 1)
    for t in peers:
        await_value(j * n_section + t)
    whole = plane(value_blocks, j)
    for k, i in enumerate(line):
        push(whole, whole, value_line_send.at[k], value_line_recv.at[z], s, i)
    push(whole, whole, value_twin_send.at[0], value_twin_recv.at[z], s, twin)
    theirs = pl.ds(pl.multiple_of((1 - c) * half, half), half)
    for k, t in enumerate(others):
        arrived(wq.at[t, theirs, :], wf_recv.at[t])
        project(k + 1)
    rest = pl.ds(1, n_section - 1)
    for k, t in enumerate(others):
        push(q_part.at[t, rest], q_got.at[s, rest], q_send.at[1, k], q_recv.at[s, 1], t, j)
    for t in others:
        arrived(q_got.at[t, 0], q_recv.at[t, 0])
        arrived(q_got.at[t, rest], q_recv.at[t, 1])
    for h in range(n_section):
        place = (h + n_section - s) % n_section
        value = q_part[s, place].astype(jnp.float32)
        for t in others:
            value = value + q_got[t, (h + n_section - t) % n_section].astype(jnp.float32)
        queries[h * BLOCK : (h + 1) * BLOCK, :] = turned(value * scaling).astype(jnp.bfloat16)

    first = ids_ref[0]
    second = ids_ref[1]
    own_header = jnp.logical_or(first == b, second == b)
    limit = jnp.where(own_header, n_section * n_line * 2, reach_ref[s])
    group = 2 * n_section
    keys_wide = group * BLOCK
    factor = 1.4426950408889634 / math.sqrt(head)
    top[...] = jnp.full(top.shape, LOW, jnp.float32)
    acc[...] = jnp.zeros(acc.shape, jnp.float32)
    ones = jnp.ones((keys_wide, head), jnp.bfloat16)
    strip = 32

    def attend(place, low, high):
        start = place * group
        numbers = start + lax.broadcasted_iota(jnp.int32, (1, keys_wide), 1) // BLOCK
        valid = (numbers == first) | (numbers == second) | (jnp.abs(numbers - b) <= limit)
        bias = jnp.where(valid, 0.0, LOW)
        keys = jnp.concatenate([key_blocks[start + n] for n in range(group)], axis=1)
        part_rows = pl.ds(low, high - low)
        scores[part_rows, :] = jnp.dot(
            queries[part_rows, :], keys, preferred_element_type=jnp.float32
        )
        for r in range(low, high, strip):
            rows = pl.ds(r, strip)
            part = scores[rows, :] * factor + bias
            before = top[rows, :]
            after = jnp.maximum(before, jnp.max(part, axis=1, keepdims=True))
            weights[rows, :] = jnp.exp2(part - after[:, 0:1]).astype(jnp.bfloat16)
            fade[rows, :] = jnp.exp2(before - after)
            top[rows, :] = after
        values = value_blocks[pl.ds(start, group)].reshape(keys_wide, head)
        gained = jnp.dot(
            weights[part_rows, :],
            jnp.concatenate([values, ones], axis=1),
            preferred_element_type=jnp.float32,
        )
        factors = fade[part_rows, :]
        for columns in (pl.ds(0, head), pl.ds(head, head)):
            acc[part_rows, columns] = (
                acc[part_rows, columns] * factors + gained[:, columns.start : columns.start + head]
            )

    def pass_on(i):
        place = (z + i) % n_line
        seq = place * 2 + c
        for t in peers:
            await_key(seq * n_section + t)
        keys = plane(key_blocks, seq)
        push(keys, keys, twin_send.at[i], key_twin_recv.at[place], s, twin)
        if i > 0:
            values = plane(value_blocks, seq)
            arrived(values, value_line_recv.at[place])
            push(values, values, value_twin_send.at[i], value_twin_recv.at[place], s, twin)

    pass_on(0)
    for i in range(n_line):
        if i + 1 < n_line:
            pass_on(i + 1)
        place = (z + i) % n_line
        seq = place * 2 + 1 - c
        arrived(plane(key_blocks, seq), key_twin_recv.at[place])
        arrived(plane(value_blocks, seq), value_twin_recv.at[place])
        if i + 1 < n_line:
            attend(place, 0, n_section * BLOCK)
    middle = n_section // 2
    for m in range(2):
        heads = range(m * middle, (m + 1) * middle)
        attend(place, heads[0] * BLOCK, (heads[-1] + 1) * BLOCK)
        for h in heads:
            rows = pl.ds(h * BLOCK, BLOCK)
            attended[s, m, :, (h - heads[0]) * head : (h - heads[0] + 1) * head] = (
                acc[rows, 0:head] / acc[rows, head : 2 * head]
            ).astype(jnp.bfloat16)
        piece = attended.at[s, m]
        for k, t in enumerate(others):
            push(piece, piece, out_send.at[m, k], out_recv.at[s, m], t, j)
    get_o.wait()

    def finish(owner, k):
        rows = pl.ds(pl.multiple_of(owner * BLOCK, BLOCK), BLOCK)
        result[rows, :] = jnp.dot(
            jnp.concatenate([attended[owner, 0], attended[owner, 1]], axis=1),
            wo[...],
            preferred_element_type=jnp.float32
        ).astype(jnp.bfloat16)
        copy = pltpu.make_async_copy(result.at[rows, :], out_ref.at[rows, :], store_sem.at[k])
        copy.start()
        return copy

    stores = [finish(s, 0)]
    for k, t in enumerate(peers):
        for m in range(2):
            arrived(attended.at[t, m], out_recv.at[t, m])
        stores.append(finish(t, k + 1))
    for copy in stores:
        copy.wait()
    for copy in pending:
        copy.wait_send()


def on_device_fused(
    n_section,
    n_seq,
    hidden,
    norm_gain,
    query_weight,
    key_weight,
    value_weight,
    output_weight,
    block_reach,
    header_ids,
):
    rows, width = hidden.shape
    head = key_weight.shape[1]
    n_line = n_seq // 2
    n_blocks = n_section * n_seq
    vmem = pl.BlockSpec(memory_space=pltpu.VMEM)
    smem = pl.BlockSpec(memory_space=pltpu.SMEM)
    anywhere = pl.BlockSpec(memory_space=pltpu.HBM)
    dma = pltpu.SemaphoreType.DMA
    bf16 = jnp.bfloat16
    f32 = jnp.float32
    return pl.pallas_call(
        functools.partial(fused, n_section, n_line),
        out_shape=jax.ShapeDtypeStruct((rows, width), bf16),
        in_specs=[anywhere, vmem, anywhere, anywhere, anywhere, anywhere, smem, smem],
        out_specs=anywhere,
        scratch_shapes=[
            pltpu.VMEM((rows, width), bf16),
            pltpu.VMEM((rows, width), bf16),
            pltpu.VMEM((n_section, width, head), bf16),
            pltpu.VMEM((width, 2 * head), bf16),
            pltpu.VMEM((n_section, 8, BLOCK), f32),
            pltpu.VMEM((n_section, 8, BLOCK), f32),
            pltpu.VMEM((n_section, BLOCK, 2 * head), bf16),
            pltpu.VMEM((n_section, BLOCK, 2 * head), bf16),
            pltpu.VMEM((n_section, n_section, BLOCK, head), bf16),
            pltpu.VMEM((n_section, n_section, BLOCK, head), bf16),
            pltpu.VMEM((n_blocks, head, BLOCK), bf16),
            pltpu.VMEM((n_blocks, BLOCK, head), bf16),
            pltpu.VMEM((n_section * BLOCK, head), bf16),
            pltpu.VMEM((n_section * BLOCK, head), f32),
            pltpu.VMEM((n_section * BLOCK, head), f32),
            pltpu.VMEM((n_section * BLOCK, 2 * head), f32),
            pltpu.VMEM((n_section * BLOCK, 2 * n_section * BLOCK), f32),
            pltpu.VMEM((n_section * BLOCK, 2 * n_section * BLOCK), bf16),
            pltpu.VMEM((n_section, 2, BLOCK, n_section // 2 * head), bf16),
            pltpu.VMEM((n_section * head, width), bf16),
            pltpu.VMEM((rows, width), bf16),
            dma((5,)),
            dma((n_section,)),
            dma((n_section - 1,)),
            dma((n_section,)),
            dma((n_section - 1,)),
            dma((n_section,)),
            dma((n_section - 1,)),
            dma((n_section,)),
            dma((n_section - 1,)),
            dma((n_section,)),
            dma((n_section - 1,)),
            dma((n_section,)),
            dma((2, n_section - 1)),
            dma((n_section, 2)),
            dma((n_line - 1,)),
            dma((n_line, n_section - 1)),
            dma((n_line,)),
            dma((n_blocks,)),
            dma((n_line,)),
            dma((n_section - 1,)),
            dma((n_line - 1,)),
            dma((n_line,)),
            dma((n_section,)),
            dma((n_line,)),
            dma((n_line,)),
            dma((2, n_section - 1)),
            dma((n_section, 2)),
            dma((n_section,)),
        ],
        compiler_params=pltpu.CompilerParams(
            collective_id=0, has_side_effects=True, vmem_limit_bytes=60 * 1024 * 1024
        ),
    )(
        hidden,
        norm_gain,
        query_weight,
        key_weight,
        value_weight,
        output_weight,
        block_reach,
        header_ids,
    )

def solution(mesh):
    n_section, n_seq = mesh.shape["section"], mesh.shape["seq"]
    if n_section * n_seq <= FUSED_BLOCKS:
        program = functools.partial(on_device_fused, n_section, n_seq)
    else:
        program = on_device
    return jax.shard_map(
        program,
        mesh=mesh,
        in_specs=(
            P("seq", "section"),
            P("section"),
            P(None, "section"),
            P("section", None),
            P("section", None),
            P(None, "section"),
            P("seq"),
            P(),
        ),
        out_specs=P("seq", "section"),
        check_vma=False,
    )
```

```python
import functools
import math

import jax
import jax.numpy as jnp
from jax import lax
from jax.experimental import pallas as pl
from jax.experimental.pallas import tpu as pltpu
from jax.sharding import PartitionSpec as P

BLOCK = 128
REACH = 2


EPSILON = 1e-05
THETA = 500000.0


def merged(value, axis, combine):
    everything = jax.tree.map(lambda part: lax.all_gather(part, axis), value)
    leading = jax.tree.map(lambda part: part[0], everything)

    def lap(k, so_far):
        return combine(so_far, jax.tree.map(lambda part: part[k], everything))

    return lax.fori_loop(1, lax.axis_size(axis), lap, leading)


def padded(cells, sides, width):
    for axis, dim in sides:
        count = lax.axis_size(axis)
        ends = count - 1
        head = lax.slice_in_dim(cells, 0, width, axis=dim)
        tail = lax.slice_in_dim(cells, cells.shape[dim] - width, cells.shape[dim], axis=dim)
        cells = jnp.concatenate(
            [
                lax.ppermute(tail, axis, [(i, (i + 1) % count) for i in range(ends)]),
                cells,
                lax.ppermute(head, axis, [((i + 1) % count, i) for i in range(ends)]),
            ],
            axis=dim,
        )
    return cells


def tables(positions, head_width):
    middle = head_width // 2
    frequency = jnp.exp(
        -(2.0 / head_width) * math.log(THETA) * jnp.arange(middle, dtype=jnp.float32)
    )
    angles = positions.astype(jnp.float32)[:, None] * frequency[None, :]
    angles = jnp.concatenate([angles, angles], axis=1)
    return (jnp.cos(angles), jnp.sin(angles))


def rotate(values, cosine_table, sine_table):
    middle = values.shape[-1] // 2
    turned = jnp.concatenate([-values[..., middle:], values[..., :middle]], axis=-1)
    return values * cosine_table + turned * sine_table


def combine_parts(earlier, later):
    first_max, first_total, first_out = earlier
    second_max, second_total, second_out = later
    overall = jnp.maximum(first_max, second_max)
    first_factor = jnp.exp(first_max - overall)
    second_factor = jnp.exp(second_max - overall)
    return (
        overall,
        first_total * first_factor + second_total * second_factor,
        first_out * first_factor[:, None] + second_out * second_factor[:, None],
    )


def on_device(
    hidden,
    norm_gain,
    query_weight,
    key_weight,
    value_weight,
    output_weight,
    block_reach,
    header_ids,
):
    row_count = hidden.shape[0]
    part_width = hidden.shape[1]
    head_width = key_weight.shape[1]
    local_blocks = row_count // BLOCK
    total_blocks = local_blocks * lax.axis_size("seq")
    seq_place = lax.axis_index("seq")
    floats = hidden.astype(jnp.float32)
    squares = lax.psum(jnp.sum(floats * floats, axis=1), "section")
    scaling = lax.rsqrt(squares / (part_width * lax.axis_size("section")) + EPSILON)
    normed_part = (floats * scaling[:, None] * norm_gain.astype(jnp.float32)[None, :]).astype(
        jnp.bfloat16
    )
    weight_rows = query_weight
    query_sum = jnp.dot(
        lax.all_gather(normed_part, "section", axis=1, tiled=True),
        weight_rows,
        preferred_element_type=jnp.float32,
    )
    key_sum, value_sum = lax.psum(
        (
            jnp.dot(normed_part, key_weight, preferred_element_type=jnp.float32),
            jnp.dot(normed_part, value_weight, preferred_element_type=jnp.float32),
        ),
        "section",
    )
    positions = seq_place * row_count + jnp.arange(row_count, dtype=jnp.int32)
    cosine_table, sine_table = tables(positions, head_width)
    queries = rotate(query_sum, cosine_table, sine_table).astype(jnp.bfloat16)
    keys_here = rotate(key_sum, cosine_table, sine_table).astype(jnp.bfloat16)
    values_here = value_sum.astype(jnp.bfloat16)
    packed = jnp.concatenate([queries, keys_here, values_here], axis=1)
    block_numbers = seq_place * local_blocks + jnp.arange(local_blocks, dtype=jnp.int32)
    select = header_ids[:, None] == block_numbers[None, :]
    shaped = packed.reshape(local_blocks, BLOCK, 3 * head_width)
    picked = jnp.einsum(
        "hb,bre->hre", select.astype(jnp.bfloat16), shaped, preferred_element_type=jnp.float32
    )
    header_pack = lax.psum(picked, "seq").astype(jnp.bfloat16).reshape(-1, 3 * head_width)
    head_queries = header_pack[:, :head_width]
    head_keys = header_pack[:, head_width : 2 * head_width]
    head_values = header_pack[:, 2 * head_width :]
    inverse_root = 1.0 / math.sqrt(head_width)
    far_scores = (
        jnp.einsum("qd,kd->qk", head_queries, keys_here, preferred_element_type=jnp.float32)
        * inverse_root
    )
    far_max = jnp.max(far_scores, axis=1)
    far_weights = jnp.exp(far_scores - far_max[:, None])
    far_total = jnp.sum(far_weights, axis=1)
    far_out = jnp.dot(
        far_weights.astype(jnp.bfloat16), values_here, preferred_element_type=jnp.float32
    )
    merged_max, merged_total, merged_out = merged(
        (far_max, far_total, far_out), "seq", combine_parts
    )
    header_result = merged_out / merged_total[:, None]
    margin_rows = REACH * BLOCK
    stacked = jnp.concatenate([keys_here, values_here], axis=1)
    extended = padded(stacked, (("seq", 0),), margin_rows)
    near_keys = extended[:, :head_width]
    near_values = extended[:, head_width:]
    extent = row_count + 2 * margin_rows
    key_blocks = seq_place * local_blocks - REACH + jnp.arange(extent, dtype=jnp.int32) // BLOCK
    query_blocks = seq_place * local_blocks + jnp.arange(row_count, dtype=jnp.int32) // BLOCK
    limits = jnp.repeat(block_reach, BLOCK)
    key_header = jnp.any(header_ids[:, None] == key_blocks[None, :], axis=0)
    allowed = (key_blocks >= 0)[None, :] & (key_blocks < total_blocks)[None, :]
    allowed = allowed & (jnp.abs(key_blocks[None, :] - query_blocks[:, None]) <= limits[:, None])
    allowed = allowed & jnp.logical_not(key_header)[None, :]
    near_scores = (
        jnp.einsum("qd,kd->qk", queries, near_keys, preferred_element_type=jnp.float32)
        * inverse_root
    )
    near_scores = jnp.where(allowed, near_scores, -jnp.inf)
    head_scores = (
        jnp.einsum("qd,kd->qk", queries, head_keys, preferred_element_type=jnp.float32)
        * inverse_root
    )
    scores = jnp.concatenate([near_scores, head_scores], axis=1)
    row_top = jnp.max(scores, axis=1)
    weights = jnp.exp(scores - row_top[:, None])
    row_sums = jnp.sum(weights, axis=1)
    joined = jnp.concatenate([near_values, head_values], axis=0)
    mixed_out = (
        jnp.dot(weights.astype(jnp.bfloat16), joined, preferred_element_type=jnp.float32)
        / row_sums[:, None]
    )
    header_local = jnp.einsum(
        "hb,hre->bre", select.astype(jnp.float32), header_result.reshape(-1, BLOCK, head_width)
    )
    is_local_header = jnp.any(select, axis=0)
    attended = jnp.where(
        is_local_header[:, None, None],
        header_local,
        mixed_out.reshape(local_blocks, BLOCK, head_width),
    )
    attended = attended.reshape(row_count, head_width).astype(jnp.bfloat16)
    weight_rows = output_weight
    result = jnp.dot(
        lax.all_gather(attended, "section", axis=1, tiled=True),
        weight_rows,
        preferred_element_type=jnp.float32,
    )
    return result.astype(jnp.bfloat16)


MESH = pl.DeviceIdType.MESH
LOW = -1e30
FUSED_BLOCKS = 64


def fused(
    n_section,
    n_line,
    hidden_ref,
    gain_ref,
    query_ref,
    key_ref,
    value_ref,
    project_ref,
    reach_ref,
    ids_ref,
    out_ref,
    x,
    scaled,
    wq,
    wkv,
    squares,
    squares_got,
    kv_part,
    kv_got,
    q_part,
    q_got,
    key_blocks,
    value_blocks,
    queries,
    top,
    fade,
    acc,
    scores,
    weights,
    attended,
    wo,
    result,
    local_sem,
    x_sem,
    w_send,
    w_recv,
    wz_send,
    wz_recv,
    wf_send,
    wf_recv,
    sq_send,
    sq_recv,
    kv_send,
    kv_recv,
    q_send,
    q_recv,
    line_send,
    plane_send,
    twin_send,
    key_recv,
    key_twin_recv,
    value_plane_send,
    value_line_send,
    value_twin_send,
    value_recv,
    value_line_recv,
    value_twin_recv,
    out_send,
    out_recv,
    store_sem,
):
    width = x.shape[1]
    half = width // 2
    head = wq.shape[2]
    s = lax.axis_index("section")
    j = lax.axis_index("seq")
    z = j // 2
    c = j % 2
    twin = z * 2 + (1 - c)
    others = [(s + k) % n_section for k in range(1, n_section)]
    line = [((z + k) % n_line) * 2 + c for k in range(1, n_line)]

    def push(src, dst, send, recv, section, seq):
        copy = pltpu.make_async_remote_copy(
            src_ref=src,
            dst_ref=dst,
            send_sem=send,
            recv_sem=recv,
            device_id=(section, seq),
            device_id_type=MESH,
        )
        copy.start()
        pending.append(copy)

    def arrived(dst, recv):
        pltpu.make_async_remote_copy(
            src_ref=dst,
            dst_ref=dst,
            send_sem=local_sem.at[4],
            recv_sem=recv,
            device_id=(s, twin),
            device_id_type=MESH,
        ).wait_recv()

    pending = []
    get_x = []
    for r in range(n_section):
        rows = pl.ds(r * BLOCK, BLOCK)
        get_x.append(pltpu.make_async_copy(hidden_ref.at[rows, :], x.at[rows, :], x_sem.at[r]))
        get_x[r].start()
    get_k = pltpu.make_async_copy(key_ref, wkv.at[:, 0:head], local_sem.at[1])
    get_v = pltpu.make_async_copy(value_ref, wkv.at[:, head : 2 * head], local_sem.at[2])
    get_q = pltpu.make_async_copy(
        query_ref.at[pl.ds(pl.multiple_of(s * width, width), width), :], wq.at[s], local_sem.at[3]
    )
    get_o = pltpu.make_async_copy(project_ref, wo, local_sem.at[0])
    get_k.start()
    get_v.start()
    get_q.start()
    get_o.start()

    barrier = pltpu.get_barrier_semaphore()
    friends = [(t, j) for t in others] + [(s, i) for i in line] + [(s, twin)]
    for friend in friends:
        pl.semaphore_signal(barrier, inc=1, device_id=friend, device_id_type=MESH)

    pl.semaphore_wait(barrier, len(friends))

    quarter = half // 2
    partner = (z + 1 - 2 * (z % 2)) * 2 + c
    mine = pl.ds(pl.multiple_of(c * half, half), half)
    near = pl.ds(pl.multiple_of(c * half + (z % 2) * quarter, quarter), quarter)
    far = pl.ds(pl.multiple_of(c * half + (1 - z % 2) * quarter, quarter), quarter)
    for k, t in enumerate(others):
        push(
            query_ref.at[
                pl.ds(
                    pl.multiple_of(t * width + c * half + (z % 2) * quarter, quarter), quarter
                ),
                :,
            ],
            wq.at[s, near, :],
            w_send.at[k],
            w_recv.at[s],
            t,
            j,
        )

    gain = gain_ref[...].astype(jnp.float32).reshape(1, width)
    for r in range(n_section):
        get_x[r].wait()
        part = x[r * BLOCK : (r + 1) * BLOCK, :].astype(jnp.float32)
        scaled[r * BLOCK : (r + 1) * BLOCK, :] = (part * gain).astype(jnp.bfloat16)
    get_k.wait()
    get_v.wait()
    kv_part[...] = (
        jnp.dot(scaled[...], wkv[...], preferred_element_type=jnp.float32)
        .astype(jnp.bfloat16)
        .reshape(kv_part.shape)
    )
    for k, t in enumerate(others):
        push(kv_part.at[t], kv_got.at[s], kv_send.at[k], kv_recv.at[s], t, j)

    for r in range(n_section):
        part = x[r * BLOCK : (r + 1) * BLOCK, :].astype(jnp.float32)
        column = jnp.sum(part * part, axis=1, keepdims=True)
        squares[r] = jnp.transpose(jnp.broadcast_to(column, (BLOCK, BLOCK)))[:8, :]
    for k, t in enumerate(others):
        push(squares.at[t], squares_got.at[s], sq_send.at[k], sq_recv.at[s], t, j)

    b = j * n_section + s
    lanes = lax.broadcasted_iota(jnp.int32, (BLOCK, head), 1)
    positions = b * BLOCK + lax.broadcasted_iota(jnp.int32, (BLOCK, head), 0)
    spots = lax.rem(lanes, head // 2).astype(jnp.float32)
    angles = positions.astype(jnp.float32) * jnp.exp(-(2.0 / head) * math.log(THETA) * spots)
    cosine = jnp.cos(angles)
    sine = jnp.where(lanes < head // 2, -1.0, 1.0) * jnp.sin(angles)

    def project(k):
        owner = (s + k) % n_section
        q_part[:, k] = (
            jnp.dot(scaled[...], wq[owner], preferred_element_type=jnp.float32)
            .astype(jnp.bfloat16)
            .reshape(n_section, BLOCK, head)
        )

    get_q.wait()
    project(0)
    for k, t in enumerate(others):
        push(q_part.at[t, 0], q_got.at[s, 0], q_send.at[0, k], q_recv.at[s, 0], t, j)
    for k, t in enumerate(others):
        arrived(wq.at[t, near, :], w_recv.at[t])
        push(wq.at[t, near, :], wq.at[t, near, :], wz_send.at[k], wz_recv.at[t], s, partner)

    def turned(values):
        return values * cosine + pltpu.roll(values, head // 2, axis=1) * sine

    for t in others:
        arrived(squares_got.at[t], sq_recv.at[t])
    sums = squares[s]
    for t in others:
        sums = sums + squares_got[t]
    scaling = lax.rsqrt(sums / (width * n_section) + EPSILON)
    scaling = jnp.transpose(jnp.broadcast_to(scaling[0:1, :], (BLOCK, BLOCK)))
    for t in others:
        arrived(kv_got.at[t], kv_recv.at[t])
    kv = kv_part[s].astype(jnp.float32)
    for t in others:
        kv = kv + kv_got[t].astype(jnp.float32)
    key_blocks[b] = jnp.transpose(turned(kv[:, :head] * scaling)).astype(jnp.bfloat16)
    value_blocks[b] = (kv[:, head:] * scaling).astype(jnp.bfloat16)

    across = s + 1 - 2 * (s % 2)
    along = (s + 2) % n_section
    corner = (across + 2) % n_section
    peers = [across, along, corner]

    def hand_key(number, send, section, seq):
        piece = key_blocks.at[number]
        push(piece, piece, send, key_recv.at[number], section, seq)

    def hand_value(number, send, section):
        piece = value_blocks.at[number]
        push(piece, piece, send, value_recv.at[number - j * n_section], section, j)

    def await_key(number):
        arrived(key_blocks.at[number], key_recv.at[number])

    def await_value(number):
        arrived(value_blocks.at[number], value_recv.at[number - j * n_section])

    def plane(blocks, seq):
        return blocks.at[pl.ds(seq * n_section, n_section)]

    def spread_key(number, slot):
        for k, t in enumerate(peers):
            hand_key(number, plane_send.at[slot, k], t, j)

    for k, i in enumerate(line):
        hand_key(b, line_send.at[k], s, i)
    for k, t in enumerate(peers):
        hand_value(b, value_plane_send.at[k], t)
    spread_key(b, 0)

    for k, t in enumerate(others):
        arrived(wq.at[t, far, :], wz_recv.at[t])
        push(wq.at[t, mine, :], wq.at[t, mine, :], wf_send.at[k], wf_recv.at[t], s, twin)
    for k, i in enumerate(line):
        number = i * n_section + s
        await_key(number)
        spread_key(number, k + 1)
    for t in peers:
        await_value(j * n_section + t)
    whole = plane(value_blocks, j)
    for k, i in enumerate(line):
        push(whole, whole, value_line_send.at[k], value_line_recv.at[z], s, i)
    push(whole, whole, value_twin_send.at[0], value_twin_recv.at[z], s, twin)
    theirs = pl.ds(pl.multiple_of((1 - c) * half, half), half)
    for k, t in enumerate(others):
        arrived(wq.at[t, theirs, :], wf_recv.at[t])
        project(k + 1)
    rest = pl.ds(1, n_section - 1)
    for k, t in enumerate(others):
        push(q_part.at[t, rest], q_got.at[s, rest], q_send.at[1, k], q_recv.at[s, 1], t, j)
    for t in others:
        arrived(q_got.at[t, 0], q_recv.at[t, 0])
        arrived(q_got.at[t, rest], q_recv.at[t, 1])
    for h in range(n_section):
        place = (h + n_section - s) % n_section
        value = q_part[s, place].astype(jnp.float32)
        for t in others:
            value = value + q_got[t, (h + n_section - t) % n_section].astype(jnp.float32)
        queries[h * BLOCK : (h + 1) * BLOCK, :] = turned(value * scaling).astype(jnp.bfloat16)

    first = ids_ref[0]
    second = ids_ref[1]
    own_header = jnp.logical_or(first == b, second == b)
    limit = jnp.where(own_header, n_section * n_line * 2, reach_ref[s])
    group = 2 * n_section
    keys_wide = group * BLOCK
    factor = 1.4426950408889634 / math.sqrt(head)
    top[...] = jnp.full(top.shape, LOW, jnp.float32)
    acc[...] = jnp.zeros(acc.shape, jnp.float32)
    ones = jnp.ones((keys_wide, head), jnp.bfloat16)
    strip = 32

    def attend(place, low, high):
        start = place * group
        numbers = start + lax.broadcasted_iota(jnp.int32, (1, keys_wide), 1) // BLOCK
        valid = (numbers == first) | (numbers == second) | (jnp.abs(numbers - b) <= limit)
        bias = jnp.where(valid, 0.0, LOW)
        keys = jnp.concatenate([key_blocks[start + n] for n in range(group)], axis=1)
        part_rows = pl.ds(low, high - low)
        scores[part_rows, :] = jnp.dot(
            queries[part_rows, :], keys, preferred_element_type=jnp.float32
        )
        for r in range(low, high, strip):
            rows = pl.ds(r, strip)
            part = scores[rows, :] * factor + bias
            before = top[rows, :]
            after = jnp.maximum(before, jnp.max(part, axis=1, keepdims=True))
            weights[rows, :] = jnp.exp2(part - after[:, 0:1]).astype(jnp.bfloat16)
            fade[rows, :] = jnp.exp2(before - after)
            top[rows, :] = after
        values = value_blocks[pl.ds(start, group)].reshape(keys_wide, head)
        gained = jnp.dot(
            weights[part_rows, :],
            jnp.concatenate([values, ones], axis=1),
            preferred_element_type=jnp.float32,
        )
        factors = fade[part_rows, :]
        for columns in (pl.ds(0, head), pl.ds(head, head)):
            acc[part_rows, columns] = (
                acc[part_rows, columns] * factors + gained[:, columns.start : columns.start + head]
            )

    def pass_on(i):
        place = (z + i) % n_line
        seq = place * 2 + c
        for t in peers:
            await_key(seq * n_section + t)
        keys = plane(key_blocks, seq)
        push(keys, keys, twin_send.at[i], key_twin_recv.at[place], s, twin)
        if i > 0:
            values = plane(value_blocks, seq)
            arrived(values, value_line_recv.at[place])
            push(values, values, value_twin_send.at[i], value_twin_recv.at[place], s, twin)

    pass_on(0)
    for i in range(n_line):
        if i == 1:
            for later in range(1, n_line):
                pass_on(later)
        place = (z + i) % n_line
        seq = place * 2 + 1 - c
        arrived(plane(key_blocks, seq), key_twin_recv.at[place])
        arrived(plane(value_blocks, seq), value_twin_recv.at[place])
        if i + 1 < n_line:
            attend(place, 0, n_section * BLOCK)
    middle = n_section // 2
    for m in range(2):
        heads = range(m * middle, (m + 1) * middle)
        attend(place, heads[0] * BLOCK, (heads[-1] + 1) * BLOCK)
        for h in heads:
            rows = pl.ds(h * BLOCK, BLOCK)
            attended[s, m, :, (h - heads[0]) * head : (h - heads[0] + 1) * head] = (
                acc[rows, 0:head] / acc[rows, head : 2 * head]
            ).astype(jnp.bfloat16)
        piece = attended.at[s, m]
        for k, t in enumerate(others):
            push(piece, piece, out_send.at[m, k], out_recv.at[s, m], t, j)
    get_o.wait()

    def finish(owner, k):
        rows = pl.ds(pl.multiple_of(owner * BLOCK, BLOCK), BLOCK)
        result[rows, :] = jnp.dot(
            jnp.concatenate([attended[owner, 0], attended[owner, 1]], axis=1),
            wo[...],
            preferred_element_type=jnp.float32
        ).astype(jnp.bfloat16)
        copy = pltpu.make_async_copy(result.at[rows, :], out_ref.at[rows, :], store_sem.at[k])
        copy.start()
        return copy

    stores = [finish(s, 0)]
    for k, t in enumerate(peers):
        for m in range(2):
            arrived(attended.at[t, m], out_recv.at[t, m])
        stores.append(finish(t, k + 1))
    for copy in stores:
        copy.wait()
    for copy in pending:
        copy.wait_send()


def on_device_fused(
    n_section,
    n_seq,
    hidden,
    norm_gain,
    query_weight,
    key_weight,
    value_weight,
    output_weight,
    block_reach,
    header_ids,
):
    rows, width = hidden.shape
    head = key_weight.shape[1]
    n_line = n_seq // 2
    n_blocks = n_section * n_seq
    vmem = pl.BlockSpec(memory_space=pltpu.VMEM)
    smem = pl.BlockSpec(memory_space=pltpu.SMEM)
    anywhere = pl.BlockSpec(memory_space=pltpu.HBM)
    dma = pltpu.SemaphoreType.DMA
    bf16 = jnp.bfloat16
    f32 = jnp.float32
    return pl.pallas_call(
        functools.partial(fused, n_section, n_line),
        out_shape=jax.ShapeDtypeStruct((rows, width), bf16),
        in_specs=[anywhere, vmem, anywhere, anywhere, anywhere, anywhere, smem, smem],
        out_specs=anywhere,
        scratch_shapes=[
            pltpu.VMEM((rows, width), bf16),
            pltpu.VMEM((rows, width), bf16),
            pltpu.VMEM((n_section, width, head), bf16),
            pltpu.VMEM((width, 2 * head), bf16),
            pltpu.VMEM((n_section, 8, BLOCK), f32),
            pltpu.VMEM((n_section, 8, BLOCK), f32),
            pltpu.VMEM((n_section, BLOCK, 2 * head), bf16),
            pltpu.VMEM((n_section, BLOCK, 2 * head), bf16),
            pltpu.VMEM((n_section, n_section, BLOCK, head), bf16),
            pltpu.VMEM((n_section, n_section, BLOCK, head), bf16),
            pltpu.VMEM((n_blocks, head, BLOCK), bf16),
            pltpu.VMEM((n_blocks, BLOCK, head), bf16),
            pltpu.VMEM((n_section * BLOCK, head), bf16),
            pltpu.VMEM((n_section * BLOCK, head), f32),
            pltpu.VMEM((n_section * BLOCK, head), f32),
            pltpu.VMEM((n_section * BLOCK, 2 * head), f32),
            pltpu.VMEM((n_section * BLOCK, 2 * n_section * BLOCK), f32),
            pltpu.VMEM((n_section * BLOCK, 2 * n_section * BLOCK), bf16),
            pltpu.VMEM((n_section, 2, BLOCK, n_section // 2 * head), bf16),
            pltpu.VMEM((n_section * head, width), bf16),
            pltpu.VMEM((rows, width), bf16),
            dma((5,)),
            dma((n_section,)),
            dma((n_section - 1,)),
            dma((n_section,)),
            dma((n_section - 1,)),
            dma((n_section,)),
            dma((n_section - 1,)),
            dma((n_section,)),
            dma((n_section - 1,)),
            dma((n_section,)),
            dma((n_section - 1,)),
            dma((n_section,)),
            dma((2, n_section - 1)),
            dma((n_section, 2)),
            dma((n_line - 1,)),
            dma((n_line, n_section - 1)),
            dma((n_line,)),
            dma((n_blocks,)),
            dma((n_line,)),
            dma((n_section - 1,)),
            dma((n_line - 1,)),
            dma((n_line,)),
            dma((n_section,)),
            dma((n_line,)),
            dma((n_line,)),
            dma((2, n_section - 1)),
            dma((n_section, 2)),
            dma((n_section,)),
        ],
        compiler_params=pltpu.CompilerParams(
            collective_id=0, has_side_effects=True, vmem_limit_bytes=60 * 1024 * 1024
        ),
    )(
        hidden,
        norm_gain,
        query_weight,
        key_weight,
        value_weight,
        output_weight,
        block_reach,
        header_ids,
    )

def solution(mesh):
    n_section, n_seq = mesh.shape["section"], mesh.shape["seq"]
    if n_section * n_seq <= FUSED_BLOCKS:
        program = functools.partial(on_device_fused, n_section, n_seq)
    else:
        program = on_device
    return jax.shard_map(
        program,
        mesh=mesh,
        in_specs=(
            P("seq", "section"),
            P("section"),
            P(None, "section"),
            P("section", None),
            P("section", None),
            P(None, "section"),
            P("seq"),
            P(),
        ),
        out_specs=P("seq", "section"),
        check_vma=False,
    )
```
